32 devices in a mesh: dom: 2 (over y), chol: 4 (over z), walk: 4 (over x, core).
Axes of the slice: x: 2, y: 2, z: 4, core: 2. Of those that a mesh axis runs over, the one named last changes fastest.
Arguments:
- chol_vectors: bfloat16 [32, 100, 1000], P('chol', None, 'walk'), may hold values from -0.0047302246 to 0.0047302246
- green_blocks: bfloat16 [8, 4, 100, 1000], P(('dom', 'walk'), 'chol'), parts along dimension 0, may hold values from -6 to 6
- phase_codes: int32 [8, 4], P(('dom', 'walk')), parts along dimension 0, may hold values from 0 to 7
- occupations: int32 [8, 4, 100], P(('dom', 'walk'), 'chol'), parts along dimension 0, may hold values from 0 to 99, each once within a row
Outputs:
- chol_grad: float32 [64, 100, 1000], P(('dom', 'chol'), None, 'walk'), parts along dimension 0
- energies: float32 [8, 4], P(('dom', 'walk'), 'chol'), parts along dimension 0
The draws below stay inside these ranges and needn't reach their ends.
There are 2 independent parts, one for each index of `dom`. The reference program is written for one: setup_inputs(seed, part) draws one part's arguments, and reference() takes and returns one part's arrays. A program takes and returns all parts, laid end to end along the dimension named above; an argument that names none is the same for every part. Nothing has to cross between parts.
Inputs may be any that keep to these rules, and one draw needn't show every extreme that they name: Each walker's row of occupations is a permutation of 0 to 99.
All inputs are finite; a program needn't handle non-finite values.
Results may differ from the reference program's by a relative error of at most 0.0029.
Values may be sent and summed in bfloat16 or wider, within the bound.
No kernel may reach another device: no remote copies, remote signals or barrier semaphores. Data moves between devices by JAX's collectives and lax.ppermute only.
A program may use at most 128 MiB of HBM per device.

```python
import jax
import jax.numpy as jnp
from jax import lax

NORB = 1000
NOCC = 100
CHOL_DEV = 8
NCHOL = 32
GW = 4
GROUPS = 4


def touch_ends(entries, rng, low, high):
    longest = entries.shape.index(max(entries.shape))
    spots = []
    for shift in (0, 1):
        where = [jax.random.randint(jax.random.fold_in(rng, axis), (), 0, length) for axis, length in enumerate(entries.shape)]
        where[longest] = (where[longest] + shift) % entries.shape[longest]
        spots.append(tuple(where))
    return entries.at[spots[0]].set(low).at[spots[1]].set(high)


def block_scale(own_key, dims, split, smallest, largest):
    def one(dim, parts):
        draws = jax.random.uniform(jax.random.fold_in(jax.random.fold_in(own_key, 6), dim), (parts,), jnp.float32, smallest / len(split), largest / len(split))
        return jnp.repeat(jnp.exp(draws), dims[dim] // parts).reshape((-1,) + (1,) * (len(dims) - dim - 1))

    level = one(*split[0])
    for cut in split[1:]:
        level = level * one(*cut)
    return level


def centred(rng, shape, spread, limit, pieces=(), kind=jnp.bfloat16):
    array = jax.random.normal(rng, shape, jnp.float32) * spread
    if len(pieces) > 0:
        array = block_scale(rng, shape, pieces, -0.22, 0.18) * array
    return jnp.clip(array, min=-limit, max=limit).astype(kind)


def setup_inputs(seed: int = 0, part: int = 0) -> dict:
    arg_keys = jax.random.split(jax.random.key(seed), 5)
    part_keys = jax.random.split(jax.random.fold_in(arg_keys[4], part), 5)
    return {
        "chol_vectors": centred(arg_keys[0], (NCHOL, NOCC, NORB), ((2.0 / (NCHOL * NOCC * NORB)) ** 0.5), 0.0047302246, ((0, 4), (2, 4))),
        "green_blocks": centred(part_keys[1], (GROUPS, GW, NOCC, NORB), 1.0, 6.0, ((0, 4), (1, 4))),
        "phase_codes": touch_ends(jax.random.randint(part_keys[2], (GROUPS, GW), 0, 8), jax.random.fold_in(part_keys[2], 1), 0, 7).astype(jnp.int32),
        "occupations": jax.vmap(lambda own: jax.random.permutation(own, NOCC))(jax.random.split(part_keys[3], GROUPS * GW)).reshape((GROUPS, GW, NOCC)).astype(jnp.int32),
    }


def reference(chol_vectors, green_blocks, phase_codes, occupations):
    walkers = GROUPS * GW
    theta = green_blocks.reshape(walkers, NOCC, NORB)
    rows = occupations.reshape(walkers, NOCC).astype(jnp.int32)
    theta = jnp.take_along_axis(theta, rows[:, :, None], axis=1)
    theta_wide = theta.astype(jnp.float32)
    weight = jnp.cos(jnp.pi * phase_codes.reshape(walkers).astype(jnp.float32) / 4.0)

    def slab_terms(block):
        tmat = jnp.einsum('gip,wjp->gwij', block.astype(jnp.float32), theta_wide)
        energy = -0.5 * jnp.einsum('gwij,gwji->w', tmat, tmat)
        cotan = (-weight[None, :, None, None] * tmat).astype(jnp.bfloat16)
        cotan = lax.optimization_barrier(cotan).astype(jnp.float32)
        grad = jnp.einsum('gwji,wjp->gip', cotan, theta_wide)
        return grad, energy

    blocks = chol_vectors.reshape(NCHOL // CHOL_DEV, CHOL_DEV, NOCC, NORB)
    grads, energy_parts = lax.map(slab_terms, blocks)
    chol_grad = grads.reshape(NCHOL, NOCC, NORB)
    energies = jnp.sum(energy_parts, axis=0).reshape(GROUPS, GW)
    return chol_grad, energies
```

```python
import functools

import jax
import jax.numpy as jnp
from jax import lax
from jax.experimental import pallas as pl
from jax.experimental.pallas import tpu as pltpu
from jax.sharding import PartitionSpec as P

LANES = 128
GRANT = 48 * 1024 * 1024


def ceil_to(value, step):
    return -(-value // step) * step


def prep_theta(occ_ref, code_ref, green_ref, out_ref, *, width, padded):
    nocc, norb = green_ref.shape
    rows = out_ref.shape[0]
    pick = (lax.broadcasted_iota(jnp.int32, (nocc, nocc), 0) == occ_ref[...]).astype(jnp.bfloat16)
    theta = lax.dot_general(pick, green_ref[...], (((0,), (0,)), ((), ())), preferred_element_type=jnp.float32)
    mine = lax.broadcasted_iota(jnp.int32, code_ref.shape, 1) == lax.axis_index("chol")
    code = jnp.sum(jnp.where(mine, code_ref[...], 0).astype(jnp.float32), axis=1, keepdims=True)
    out_ref[...] = jnp.zeros_like(out_ref)
    for k in range(norb // width):
        out_ref[:nocc, padded * k:padded * k + width] = theta[:, width * k:width * (k + 1)].astype(jnp.bfloat16)
    out_ref[:, width:width + 1] = jnp.broadcast_to(code, (rows, 1)).astype(jnp.bfloat16)


def prep_chol(chol_ref, same_ref, other_ref):
    half, nocc = same_ref.shape[0], chol_ref.shape[1]
    width = chol_ref.shape[2]
    h = lax.rem(lax.axis_index("walk"), 2)
    for ref, start in ((same_ref, h * half), (other_ref, (1 - h) * half)):
        ref[...] = jnp.zeros_like(ref)
        for g in range(half):
            ref[g, :nocc, :width] = chol_ref[start + g]


def main(*refs, walkers, half, rows, width, padded):
    thetas, refs = refs[:walkers], refs[walkers:]
    chols, refs = refs[:4], refs[4:]
    own_ref, core_ref, xsame_ref, xother_ref, energy_ref, theta_s, chol_s, cotan_s = refs
    k = lax.axis_index("walk")
    theta_s[...] = jnp.zeros_like(theta_s)
    chol_s[...] = jnp.zeros_like(chol_s)
    for w in range(walkers):
        theta_s[w * LANES:w * LANES + rows, :] = thetas[w][...]
    for s in range(4):
        place = pl.ds(pl.multiple_of((k ^ s) * padded, padded), padded)
        for g in range(half):
            chol_s[g * LANES:g * LANES + rows, place] = chols[s][g]
    tmat = lax.dot_general(
        theta_s[...], chol_s[...], (((1,), (1,)), ((), ())), preferred_element_type=jnp.float32
    )
    for w in range(walkers):
        code = thetas[w][0:8, padded - LANES:padded].astype(jnp.float32)
        lane = lax.broadcasted_iota(jnp.int32, (8, LANES), 1) == width - (padded - LANES)
        code = jnp.sum(jnp.where(lane, code, 0.0), axis=1, keepdims=True)[0:1]
        weight = jnp.cos(jnp.pi * code / 4.0)
        total = jnp.zeros((LANES, LANES), jnp.float32)
        for g in range(half):
            block = tmat[w * LANES:(w + 1) * LANES, g * LANES:(g + 1) * LANES]
            total += block * block.T
            cotan_s[g * LANES:(g + 1) * LANES, w * LANES:(w + 1) * LANES] = (-weight * block).astype(jnp.bfloat16)
        energy_ref[w:w + 1, :] = -0.5 * jnp.sum(total, axis=0, keepdims=True)
    for ref, s in ((xsame_ref, 2), (xother_ref, 3), (core_ref, 1), (own_ref, 0)):
        place = pl.ds(pl.multiple_of((k ^ s) * padded, padded), padded)
        grad = jnp.dot(cotan_s[...], theta_s[:, place], preferred_element_type=jnp.float32)
        for g in range(half):
            ref[g] = grad[g * LANES:g * LANES + rows].astype(ref.dtype)


def finish(own_ref, core_ref, xsame_ref, xother_ref, out_ref):
    half = own_ref.shape[0]
    nocc, width = out_ref.shape[1:]
    h = lax.rem(lax.axis_index("walk"), 2)
    for g in range(half):
        out_ref[h * half + g] = (own_ref[g] + xsame_ref[g].astype(jnp.float32))[:nocc, :width]
        out_ref[(1 - h) * half + g] = (core_ref[g] + xother_ref[g].astype(jnp.float32))[:nocc, :width]


def call(kernel, outs, *operands, scratch=()):
    return pl.pallas_call(
        kernel,
        out_shape=outs,
        in_specs=[pl.BlockSpec(memory_space=pltpu.VMEM)] * len(operands),
        out_specs=jax.tree.map(lambda _: pl.BlockSpec(memory_space=pltpu.VMEM), outs),
        scratch_shapes=scratch,
        compiler_params=pltpu.CompilerParams(vmem_limit_bytes=GRANT),
    )(*operands)


def swap(x, axis, size, flip):
    return lax.ppermute(x, axis, [(i, i ^ flip) for i in range(size)])


def body(chol_vectors, green_blocks, phase_codes, occupations, *, nchol, nwalk):
    gdev, nocc, width = chol_vectors.shape
    norb = green_blocks.shape[3]
    half = gdev // 2
    rows = ceil_to(nocc, 8)
    padded = ceil_to(width, LANES)
    bf16, f32 = jnp.bfloat16, jnp.float32

    theta = call(
        functools.partial(prep_theta, width=width, padded=padded),
        jax.ShapeDtypeStruct((rows, padded * nwalk), bf16),
        occupations.reshape(1, nocc),
        phase_codes,
        green_blocks.reshape(nocc, norb),
    )
    piece = jax.ShapeDtypeStruct((half, rows, padded), bf16)
    same, other = call(prep_chol, (piece, piece), chol_vectors)

    thetas = [theta] + [swap(theta, "chol", nchol, d) for d in range(1, nchol)]
    chols = [same, swap(other, "walk", nwalk, 1), swap(same, "walk", nwalk, 2), swap(other, "walk", nwalk, 3)]
    partners = [swap(t, "walk", nwalk, 1) for t in thetas]

    wide = jax.ShapeDtypeStruct((half, rows, padded), f32)
    step = 4
    grads = None
    energy = [[], []]
    for first in range(0, nchol, step):
        group = thetas[first:first + step] + partners[first:first + step]
        walkers = len(group)
        last = nchol <= step
        kind = piece if last else wide
        *terms, e = call(
            functools.partial(main, walkers=walkers, half=half, rows=rows, width=width, padded=padded),
            (wide, wide, kind, kind, jax.ShapeDtypeStruct((walkers, LANES), f32)),
            *group,
            *chols,
            scratch=[
                pltpu.VMEM((walkers * LANES, padded * nwalk), bf16),
                pltpu.VMEM((half * LANES, padded * nwalk), bf16),
                pltpu.VMEM((half * LANES, walkers * LANES), bf16),
            ],
        )
        grads = terms if grads is None else [a + b for a, b in zip(grads, terms)]
        energy[0].append(e[:walkers // 2])
        energy[1].append(e[walkers // 2:])
    own, core, xsame, xother = grads
    xsame = swap(xsame.astype(bf16), "walk", nwalk, 2)
    xother = swap(xother.astype(bf16), "walk", nwalk, 3)
    core = swap(core, "walk", nwalk, 1)

    mine, theirs = (jnp.concatenate(e) if len(e) > 1 else e[0] for e in energy)
    part = mine + swap(theirs, "walk", nwalk, 1)
    flip = nchol // 2
    while flip:
        part = part[:flip] + swap(part[flip:], "chol", nchol, flip)
        flip //= 2
    energies = jnp.sum(part).reshape(1, 1)

    chol_grad = call(finish, jax.ShapeDtypeStruct((gdev, nocc, width), f32), own, core, xsame, xother)
    return chol_grad, energies


def solution(mesh):
    placed = (
        P("chol", None, "walk"),
        P(("dom", "walk"), "chol", None, None),
        P(("dom", "walk"), None),
        P(("dom", "walk"), "chol", None),
    )
    return jax.shard_map(
        functools.partial(body, nchol=mesh.shape["chol"], nwalk=mesh.shape["walk"]),
        mesh=mesh,
        in_specs=placed,
        out_specs=(P(("dom", "chol"), None, "walk"), P(("dom", "walk"), "chol")),
        check_vma=False,
    )
```

```python
import functools

import jax
import jax.numpy as jnp
from jax import lax
from jax.experimental import pallas as pl
from jax.experimental.pallas import tpu as pltpu
from jax.sharding import PartitionSpec as P

LANES = 128
GRANT = 16 * 1024 * 1024
HBM = pltpu.MemorySpace.HBM
VMEM = pltpu.MemorySpace.VMEM
bf16, f32 = jnp.bfloat16, jnp.float32


def ceil_to(value, step):
    return -(-value // step) * step


def prep_theta(occ_hbm, code_hbm, green_hbm, out_ref, occ_ref, code_ref, green_ref, sems, *, width, padded):
    copies = [
        pltpu.make_async_copy(src, dst, sems.at[i])
        for i, (src, dst) in enumerate(((occ_hbm, occ_ref), (code_hbm, code_ref), (green_hbm, green_ref)))
    ]
    for copy in copies:
        copy.start()
    out_ref[...] = jnp.zeros_like(out_ref)
    for copy in copies:
        copy.wait()
    nocc, norb = green_ref.shape
    rows = out_ref.shape[0]
    pick = (lax.broadcasted_iota(jnp.int32, (nocc, nocc), 0) == occ_ref[...]).astype(bf16)
    theta = lax.dot_general(pick, green_ref[...], (((0,), (0,)), ((), ())), preferred_element_type=f32)
    mine = lax.broadcasted_iota(jnp.int32, code_ref.shape, 1) == lax.axis_index("chol")
    code = jnp.sum(jnp.where(mine, code_ref[...], 0).astype(f32), axis=1, keepdims=True)
    for k in range(norb // width):
        out_ref[:nocc, padded * k:padded * k + width] = theta[:, width * k:width * (k + 1)].astype(bf16)
    out_ref[:, width:width + 1] = jnp.broadcast_to(code, (rows, 1)).astype(bf16)


def prep_chol(chol_ref, theta_ref, cross_ref, pair_ref):
    gdev, nocc, width = chol_ref.shape
    half = gdev // 2
    padded = cross_ref.shape[2] // half
    h = lax.rem(lax.axis_index("walk"), 2)
    cross_ref[...] = jnp.zeros_like(cross_ref)
    for i, start in enumerate((h * half, (1 - h) * half)):
        for g in range(half):
            cross_ref[i, :nocc, g * padded:g * padded + width] = chol_ref[start + g]
    pair_ref[0] = theta_ref[...]
    pair_ref[1] = jnp.zeros(pair_ref.shape[1:], pair_ref.dtype)
    pair_ref[1, :nocc] = cross_ref[1]


def second(pair_ref, out_ref):
    out_ref[...] = jnp.zeros_like(out_ref)
    out_ref[:pair_ref.shape[1]] = pair_ref[1]


def join(a_ref, b_ref, out_ref):
    out_ref[...] = a_ref[...] + b_ref[...]


def place_chol(own_ref, pair_ref, same_ref, other_ref, out_ref, *, half, rows, padded):
    out_ref[...] = jnp.zeros_like(out_ref)
    for s, ref in enumerate((own_ref.at[0], pair_ref.at[1], same_ref.at[0], other_ref)):
        for g in range(half):
            block = ref[:, g * padded:(g + 1) * padded]
            out_ref[g * LANES:g * LANES + block.shape[0], column(s, padded)] = block


def weights(theta, width, padded):
    code = theta[0:8, padded - LANES:padded].astype(f32)
    lane = lax.broadcasted_iota(jnp.int32, (8, LANES), 1) == width - (padded - LANES)
    code = jnp.sum(jnp.where(lane, code, 0.0), axis=1, keepdims=True)[0:1]
    return jnp.cos(jnp.pi * code / 4.0)


def column(s, padded):
    return pl.ds(pl.multiple_of((lax.axis_index("walk") ^ s) * padded, padded), padded)


def place_theta(thetas, theta_s):
    theta_s[...] = jnp.zeros_like(theta_s)
    for w, ref in enumerate(thetas):
        theta = ref[0] if len(ref.shape) == 3 else ref[...]
        theta_s[w * LANES:w * LANES + theta.shape[0], :] = theta


def first_walkers(*refs, walkers, half, rows, width, padded):
    *thetas, chol_s, own_ref, core_ref, same_ref, other_ref, energy_ref, theta_s, cotan_s = refs
    place_theta(thetas, theta_s)
    tmat = lax.dot_general(theta_s[...], chol_s[...], (((1,), (1,)), ((), ())), preferred_element_type=f32)
    for w in range(walkers):
        weight = weights(theta_s[w * LANES:w * LANES + 16, :], width, padded)
        total = jnp.zeros((LANES, LANES), f32)
        for g in range(half):
            block = tmat[w * LANES:(w + 1) * LANES, g * LANES:(g + 1) * LANES]
            total += block * block.T
            cotan_s[g * LANES:(g + 1) * LANES, w * LANES:(w + 1) * LANES] = (-weight * block).astype(bf16)
        energy_ref[w:w + 1, :] = -0.5 * jnp.sum(total, axis=0, keepdims=True)
    for s, ref in enumerate((own_ref, core_ref, same_ref, other_ref)):
        ref[...] = jnp.dot(cotan_s[...], theta_s[:, column(s, padded)], preferred_element_type=f32)


def last_walkers(
    mine, theirs, chol_s, same_part, other_part, same_ref, other_ref, tmat_ref, theta_s, cotan_s,
    *, walkers, half, rows, width, padded
):
    place_theta([mine, theirs], theta_s)
    tmat = lax.dot_general(theta_s[...], chol_s[...], (((1,), (1,)), ((), ())), preferred_element_type=f32)
    tmat_ref[...] = tmat
    for w in range(walkers):
        weight = weights(theta_s[w * LANES:w * LANES + 16, :], width, padded)
        for g in range(half):
            block = tmat[w * LANES:(w + 1) * LANES, g * LANES:(g + 1) * LANES]
            cotan_s[g * LANES:(g + 1) * LANES, w * LANES:(w + 1) * LANES] = (-weight * block).astype(bf16)
    for ref, part, s in ((same_ref, same_part, 2), (other_ref, other_part, 3)):
        grad = part[...] + jnp.dot(cotan_s[...], theta_s[:, column(s, padded)], preferred_element_type=f32)
        for g in range(half):
            ref[g] = grad[g * LANES:g * LANES + rows].astype(bf16)


def chip_walkers(
    tmat_ref, theta_s, cotan_s, own_part, core_part, first_ref, own_ref, core_ref, energy_ref,
    *, nocc, half, rows, padded
):
    for ref, part, s in ((core_ref, core_part, 1), (own_ref, own_part, 0)):
        grad = part[...] + jnp.dot(cotan_s[...], theta_s[:, column(s, padded)], preferred_element_type=f32)
        for g in range(half):
            ref[g] = grad[g * LANES:g * LANES + rows]
    early = first_ref.shape[0] // 2
    for w in range(2 * early):
        energy = first_ref[w:w + 1, :]
        if w < early:
            energy_ref[w:w + 1, :] = energy
        else:
            core_ref[w - early, nocc:nocc + 1, :LANES] = energy
    for w in range(2):
        total = jnp.zeros((LANES, LANES), f32)
        for g in range(half):
            block = tmat_ref[w * LANES:(w + 1) * LANES, g * LANES:(g + 1) * LANES]
            total += block * block.T
        energy = -0.5 * jnp.sum(total, axis=0, keepdims=True)
        if w == 0:
            energy_ref[early:early + 1, :] = energy
        else:
            core_ref[early, nocc:nocc + 1, :LANES] = energy


def pick_energies(energy_ref, core_ref, *out_refs, nocc):
    for w, ref in enumerate(out_refs):
        ref[...] = energy_ref[w:w + 1, :] + core_ref[w, nocc:nocc + 1, :LANES]


def finish(*refs):
    *refs, out_hbm, energy_hbm, out_ref, energy_ref, sems = refs
    own_ref, same_ref, other_ref, core_ref, *energy_refs = refs
    half, rows = own_ref.shape[:2]
    nocc, gdev, width = out_ref.shape
    h = lax.rem(lax.axis_index("walk"), 2)
    energy = sum(ref[...] for ref in energy_refs)
    energy_ref[...] = jnp.sum(energy, axis=1, keepdims=True)
    copies = [pltpu.make_async_copy(energy_ref, energy_hbm, sems.at[0])]
    copies[0].start()
    for n, start in enumerate(range(0, rows, 32), start=1):
        stop = min(start + 32, rows)
        mine = own_ref[:, start:stop, :] + same_ref[:, start:stop, :].astype(f32)
        theirs = core_ref[:half, start:stop, :] + other_ref[:, start:stop, :].astype(f32)
        low = jnp.where(h == 0, mine, theirs)
        high = jnp.where(h == 0, theirs, mine)
        both = jnp.swapaxes(jnp.concatenate([low, high], axis=0), 0, 1)
        stop = min(stop, nocc)
        out_ref[start:stop] = both[:stop - start, :, :width]
        copies.append(pltpu.make_async_copy(out_ref.at[start:stop], out_hbm.at[start:stop], sems.at[n]))
        copies[-1].start()
    for copy in copies:
        copy.wait()


def call(kernel, outs, *operands, scratch=(), ins=VMEM, out=VMEM, grant=GRANT):
    return pl.pallas_call(
        kernel,
        out_shape=outs,
        in_specs=[pl.BlockSpec(memory_space=ins)] * len(operands),
        out_specs=jax.tree.map(lambda _: pl.BlockSpec(memory_space=out), outs),
        scratch_shapes=scratch,
        compiler_params=pltpu.CompilerParams(vmem_limit_bytes=grant),
    )(*operands)


def body(chol_vectors, green_blocks, phase_codes, occupations, *, nchol, nwalk):
    gdev, nocc, width = chol_vectors.shape
    norb = green_blocks.shape[3]
    half = gdev // 2
    rows = ceil_to(nocc + 1, 8)
    padded = ceil_to(width, LANES)
    wide = padded * nwalk
    sizes = dict(half=half, rows=rows, padded=padded)

    def swap(x, flip):
        return lax.ppermute(x, "walk", [(i, i ^ flip) for i in range(nwalk)])

    def turn(x, pairs):
        return lax.ppermute(x, "chol", pairs)

    def struct(*shape, dtype=bf16):
        return jax.ShapeDtypeStruct(shape, dtype)

    theta = call(
        functools.partial(prep_theta, width=width, padded=padded),
        struct(rows, wide),
        occupations.reshape(1, nocc),
        phase_codes,
        green_blocks.reshape(nocc, norb),
        scratch=[
            pltpu.VMEM((1, nocc), jnp.int32),
            pltpu.VMEM(phase_codes.shape, jnp.int32),
            pltpu.VMEM((nocc, norb), bf16),
            pltpu.SemaphoreType.DMA((3,)),
        ],
        ins=HBM,
    )
    block = struct(rows, wide)
    cross, pair = call(prep_chol, (struct(2, nocc, wide), struct(2, rows, wide)), chol_vectors, theta)

    if nchol == 4:
        there = [(0, 2), (2, 3), (3, 1), (1, 0)]
        back = [(b, a) for a, b in there]
        paths = [there, back, [(i, 3 - i) for i in range(4)]]
        first = turn(theta, there)
        early = [first, turn(theta, back)]
        last = turn(theta, [(1, 2), (2, 1)]), turn(first, [(1, 0), (2, 3)])
    else:
        paths = [[(i, (i + d) % nchol) for i in range(nchol)] for d in range(1, nchol)]
        *early, last = [turn(theta, path) for path in paths]

    paired = swap(pair, 1)
    crossed = swap(cross, 2)
    chol = call(
        functools.partial(place_chol, **sizes),
        struct(half * LANES, wide),
        cross,
        paired,
        crossed,
        swap(call(second, block, crossed), 1),
    )
    term = struct(half * LANES, padded, dtype=f32)
    mine = [theta] + early
    theirs = [paired] + [swap(t, 1) for t in early]
    grads, energies = None, []
    for start in range(0, nchol - 1, 3):
        group = mine[start:start + 3] + theirs[start:start + 3]
        walkers = len(group)
        *terms, energy = call(
            functools.partial(first_walkers, walkers=walkers, width=width, **sizes),
            (term,) * 4 + (struct(walkers, LANES, dtype=f32),),
            *group,
            chol,
            scratch=[pltpu.VMEM((walkers * LANES, wide), bf16), pltpu.VMEM((half * LANES, walkers * LANES), bf16)],
        )
        grads = terms if grads is None else [a + b for a, b in zip(grads, terms)]
        energies += [(energy[:walkers // 2], energy[walkers // 2:])]
    if len(energies) > 1:
        energy = jnp.concatenate([e[i] for i in (0, 1) for e in energies])
    if nchol == 4:
        held = last
        last = call(join, block, *held)

    walkers = 2
    same, other, tmat, theta_s, cotan_s = call(
        functools.partial(last_walkers, walkers=walkers, width=width, **sizes),
        (
            struct(half, rows, padded),
            struct(half, rows, padded),
            struct(walkers * LANES, half * LANES, dtype=f32),
            struct(walkers * LANES, wide),
            struct(half * LANES, walkers * LANES),
        ),
        last,
        swap(last, 1),
        chol,
        grads[2],
        grads[3],
    )
    same, other = swap(same, 2), swap(other, 3)
    tall = max(half, nchol)
    own, core, energy = call(
        functools.partial(chip_walkers, nocc=nocc, **sizes),
        (struct(half, rows, padded, dtype=f32), struct(tall, rows, padded, dtype=f32), struct(nchol, LANES, dtype=f32)),
        tmat,
        theta_s,
        cotan_s,
        grads[0],
        grads[1],
        energy,
    )
    core = swap(core, 1)
    part, *parts = call(
        functools.partial(pick_energies, nocc=nocc), (struct(1, LANES, dtype=f32),) * nchol, energy, core
    )
    parts = [turn(p, [(b, a) for a, b in path]) for p, path in zip(parts, paths)]
    chol_grad, energies = call(
        finish,
        (struct(nocc, gdev, width, dtype=f32), struct(1, 1, dtype=f32)),
        own,
        same,
        other,
        core,
        part,
        *parts,
        out=HBM,
        scratch=[
            pltpu.VMEM((nocc, gdev, width), f32),
            pltpu.VMEM((1, 1), f32),
            pltpu.SemaphoreType.DMA((1 - (-rows // 32),)),
        ],
    )
    return jnp.swapaxes(chol_grad, 0, 1), energies


def solution(mesh):
    placed = (
        P("chol", None, "walk"),
        P(("dom", "walk"), "chol", None, None),
        P(("dom", "walk"), None),
        P(("dom", "walk"), "chol", None),
    )
    return jax.shard_map(
        functools.partial(body, nchol=mesh.shape["chol"], nwalk=mesh.shape["walk"]),
        mesh=mesh,
        in_specs=placed,
        out_specs=(P(("dom", "chol"), None, "walk"), P(("dom", "walk"), "chol")),
        check_vma=False,
    )
```

```python
import functools

import jax
import jax.numpy as jnp
from jax import lax
from jax.experimental import pallas as pl
from jax.experimental.pallas import tpu as pltpu
from jax.sharding import PartitionSpec as P

LANES = 128
GRANT = 16 * 1024 * 1024
PREP = 56 * 1024 * 1024
HBM = pltpu.MemorySpace.HBM
VMEM = pltpu.MemorySpace.VMEM
bf16, f32 = jnp.bfloat16, jnp.float32


def ceil_to(value, step):
    return -(-value // step) * step


def prep_theta(occ_hbm, green_hbm, out_ref, occ_ref, green_ref, sems, *, width, padded):
    copies = [pltpu.make_async_copy(green_hbm, green_ref, sems.at[0]), pltpu.make_async_copy(occ_hbm, occ_ref, sems.at[1])]
    for copy in copies:
        copy.start()
    out_ref[...] = jnp.zeros_like(out_ref)
    nocc, norb = green_ref.shape
    fold = norb // width // 2
    copies[1].wait()
    pick = (lax.broadcasted_iota(jnp.int32, (nocc, nocc), 0) == occ_ref[...]).astype(bf16)
    copies[0].wait()
    theta = lax.dot_general(pick, green_ref[...], (((0,), (0,)), ((), ())), preferred_element_type=f32)
    for k in range(norb // width):
        row, lane = k // fold * nocc, k % fold * padded
        out_ref[row:row + nocc, lane:lane + width] = theta[:, width * k:width * (k + 1)].astype(bf16)


def prep_chol(chol_ref, theta_ref, code_ref, pair_ref):
    gdev, nocc, width = chol_ref.shape
    half = gdev // 2
    padded = pair_ref.shape[2] // (half // 2)
    pair_ref[0] = theta_ref[...]
    pair_ref[1] = jnp.zeros(pair_ref.shape[1:], bf16)
    fold_half(chol_ref, pair_ref.at[1], 1 - lax.rem(lax.axis_index("walk"), 2), padded)
    nchol = code_ref.shape[1]
    shape = (ceil_to(nchol, 8), nchol)
    diagonal = lax.broadcasted_iota(jnp.int32, shape, 0) == lax.broadcasted_iota(jnp.int32, shape, 1)
    codes = jnp.sum(jnp.where(diagonal, code_ref[...], 0).astype(f32), axis=1, keepdims=True)
    lane = pair_ref.shape[2] - padded + width
    pair_ref[1, :shape[0], lane:lane + 1] = codes.astype(bf16)


def fold_half(chol_ref, out_ref, which, padded):
    gdev, nocc, width = chol_ref.shape
    half = gdev // 2
    for g in range(half):
        row, lane = g // (half // 2) * nocc, g % (half // 2) * padded
        out_ref[row:row + nocc, lane:lane + width] = chol_ref[which * half + g]


def relay(crossed_ref, out_ref, *, padded):
    out_ref[...] = jnp.zeros_like(out_ref)
    fold_half(crossed_ref, out_ref, 1 - lax.rem(lax.axis_index("walk"), 2), padded)


def join(a_ref, b_ref, out_ref):
    out_ref[...] = a_ref[...] + b_ref[...]


def place_chol(
    own_ref, pair_ref, same_ref, other_ref, code_ref, out_ref, weight_ref, *, sources, half, nocc, width, padded
):
    out_ref[...] = jnp.zeros_like(out_ref)
    h = lax.rem(lax.axis_index("walk"), 2)
    for g in range(half):
        row, lane = g // (half // 2) * nocc, g % (half // 2) * padded
        rows = slice(g * LANES, g * LANES + nocc)
        for s, ref in ((0, own_ref), (2, same_ref)):
            out_ref[rows, column(s, padded)] = jnp.pad(ref[h * half + g], ((0, 0), (0, padded - width)))
        for s, ref in ((1, pair_ref.at[1]), (3, other_ref)):
            out_ref[rows, column(s, padded)] = ref[row:row + nocc, lane:lane + padded]
    nchol = code_ref.shape[1]
    me = lax.axis_index("chol")
    lane = pair_ref.shape[2] - padded + width
    theirs = pair_ref[1, :ceil_to(nchol, 16), lane:lane + 1].astype(f32)
    mine = code_ref[...].astype(f32)
    codes = jnp.zeros(weight_ref.shape, f32)
    at = lax.broadcasted_iota(jnp.int32, codes.shape, 0)
    for n, path in enumerate(sources):
        source = sum(jnp.where(me == i, s, 0) for i, s in enumerate(path))
        for group, (values, axis) in enumerate(((mine, 1), (theirs, 0))):
            here = lax.broadcasted_iota(jnp.int32, values.shape, axis) == source
            code = jnp.sum(jnp.where(here, values, 0.0), axis=axis, keepdims=True)
            codes = jnp.where(at == group * nchol + n, code, codes)
    weight_ref[...] = -jnp.cos(jnp.pi * codes / 4.0)


def column(s, padded):
    return pl.ds(pl.multiple_of((lax.axis_index("walk") ^ s) * padded, padded), padded)


def place_theta(thetas, theta_s, nocc):
    theta_s[...] = jnp.zeros_like(theta_s)
    for w, ref in enumerate(thetas):
        theta = ref[0] if len(ref.shape) == 3 else ref[...]
        wide = theta.shape[1]
        for i in range(2):
            theta_s[w * LANES:w * LANES + nocc, i * wide:(i + 1) * wide] = theta[i * nocc:(i + 1) * nocc]


def first_walkers(*refs, first, walkers, half, nocc, padded):
    *thetas, chol_s, weight_ref, own_ref, core_ref, same_ref, other_ref, energy_ref, theta_s, cotan_s = refs
    place_theta(thetas, theta_s, nocc)
    tmat = lax.dot_general(theta_s[...], chol_s[...], (((1,), (1,)), ((), ())), preferred_element_type=f32)
    n = walkers // 2
    for w in range(walkers):
        row = w // n * (weight_ref.shape[0] // 2) + first + w % n
        weight = weight_ref[row:row + 1, :]
        total = jnp.zeros((LANES, LANES), f32)
        for g in range(half):
            block = tmat[w * LANES:(w + 1) * LANES, g * LANES:(g + 1) * LANES]
            total += block * block.T
            cotan_s[g * LANES:(g + 1) * LANES, w * LANES:(w + 1) * LANES] = (weight * block).astype(bf16)
        energy_ref[w:w + 1, :] = -0.5 * jnp.sum(total, axis=0, keepdims=True)
    for s, ref in enumerate((own_ref, core_ref, same_ref, other_ref)):
        ref[...] = jnp.dot(cotan_s[...], theta_s[:, column(s, padded)], preferred_element_type=f32)


def last_walkers(
    mine, theirs, chol_s, weight_ref, same_part, other_part, same_ref, other_ref, tmat_ref, theta_s, cotan_s,
    *, half, nocc, padded
):
    place_theta([mine, theirs], theta_s, nocc)
    tmat = lax.dot_general(theta_s[...], chol_s[...], (((1,), (1,)), ((), ())), preferred_element_type=f32)
    tmat_ref[...] = tmat
    for w in range(2):
        row = (w + 1) * (weight_ref.shape[0] // 2) - 1
        weight = weight_ref[row:row + 1, :]
        for g in range(half):
            block = tmat[w * LANES:(w + 1) * LANES, g * LANES:(g + 1) * LANES]
            cotan_s[g * LANES:(g + 1) * LANES, w * LANES:(w + 1) * LANES] = (weight * block).astype(bf16)
    for ref, part, s in ((same_ref, same_part, 2), (other_ref, other_part, 3)):
        grad = part[...] + jnp.dot(cotan_s[...], theta_s[:, column(s, padded)], preferred_element_type=f32)
        store_grad(grad, ref, half, nocc)


def store_grad(grad, ref, half, nocc):
    for g in range(half):
        if len(ref.shape) == 2:
            ref[g * nocc:(g + 1) * nocc] = grad[g * LANES:g * LANES + nocc].astype(ref.dtype)
        else:
            ref[g] = grad[g * LANES:g * LANES + ref.shape[1]].astype(ref.dtype)


def chip_walkers(
    tmat_ref, theta_s, cotan_s, own_part, core_part, first_ref, own_ref, core_ref, energy_ref,
    *, nocc, half, rows, padded
):
    for ref, part, s in ((core_ref, core_part, 1), (own_ref, own_part, 0)):
        grad = part[...] + jnp.dot(cotan_s[...], theta_s[:, column(s, padded)], preferred_element_type=f32)
        for g in range(half):
            ref[g] = grad[g * LANES:g * LANES + rows]
    early = first_ref.shape[0] // 2
    for w in range(2 * early):
        energy = first_ref[w:w + 1, :]
        if w < early:
            energy_ref[w:w + 1, :] = energy
        else:
            core_ref[w - early, nocc:nocc + 1, :LANES] = energy
    for w in range(2):
        total = jnp.zeros((LANES, LANES), f32)
        for g in range(half):
            block = tmat_ref[w * LANES:(w + 1) * LANES, g * LANES:(g + 1) * LANES]
            total += block * block.T
        energy = -0.5 * jnp.sum(total, axis=0, keepdims=True)
        if w == 0:
            energy_ref[early:early + 1, :] = energy
        else:
            core_ref[early, nocc:nocc + 1, :LANES] = energy


def pick_energies(energy_ref, core_ref, *out_refs, nocc):
    for w, ref in enumerate(out_refs):
        ref[...] = energy_ref[w:w + 1, :] + core_ref[w, nocc:nocc + 1, :LANES]


def finish(*refs):
    *refs, out_hbm, energy_hbm, out_ref, energy_ref, sems = refs
    own_ref, same_ref, other_ref, core_ref, *energy_refs = refs
    half, rows = own_ref.shape[:2]
    nocc, gdev, width = out_ref.shape
    h = lax.rem(lax.axis_index("walk"), 2)
    energy = sum(ref[...] for ref in energy_refs)
    energy_ref[...] = jnp.sum(energy, axis=1, keepdims=True)
    copies = [pltpu.make_async_copy(energy_ref, energy_hbm, sems.at[0])]
    copies[0].start()
    for n, start in enumerate(range(0, nocc, 32), start=1):
        stop = min(start + 32, nocc)

        def arrived(ref):
            return jnp.stack([ref[g * nocc + start:g * nocc + stop, :].astype(f32) for g in range(half)])

        mine = own_ref[:, start:stop, :] + arrived(same_ref)
        theirs = core_ref[:half, start:stop, :] + arrived(other_ref)
        low = jnp.where(h == 0, mine, theirs)
        high = jnp.where(h == 0, theirs, mine)
        both = jnp.swapaxes(jnp.concatenate([low, high], axis=0), 0, 1)
        out_ref[start:stop] = both[:, :, :width]
        copies.append(pltpu.make_async_copy(out_ref.at[start:stop], out_hbm.at[start:stop], sems.at[n]))
        copies[-1].start()
    for copy in copies:
        copy.wait()


def call(kernel, outs, *operands, scratch=(), ins=VMEM, out=VMEM, grant=GRANT):
    return pl.pallas_call(
        kernel,
        out_shape=outs,
        in_specs=[pl.BlockSpec(memory_space=ins)] * len(operands),
        out_specs=jax.tree.map(lambda _: pl.BlockSpec(memory_space=out), outs),
        scratch_shapes=scratch,
        compiler_params=pltpu.CompilerParams(vmem_limit_bytes=grant),
    )(*operands)


def body(chol_vectors, green_blocks, phase_codes, occupations, *, nchol, nwalk):
    gdev, nocc, width = chol_vectors.shape
    norb = green_blocks.shape[3]
    half = gdev // 2
    rows = ceil_to(nocc + 1, 8)
    padded = ceil_to(width, LANES)
    wide = padded * nwalk
    sizes = dict(half=half, padded=padded)

    def swap(x, flip):
        return lax.ppermute(x, "walk", [(i, i ^ flip) for i in range(nwalk)])

    def turn(x, pairs):
        return lax.ppermute(x, "chol", pairs)

    def struct(*shape, dtype=bf16):
        return jax.ShapeDtypeStruct(shape, dtype)

    block = struct(2 * nocc, wide // 2)
    theta = call(
        functools.partial(prep_theta, width=width, padded=padded),
        pltpu.VMEM(block.shape, bf16),
        occupations.reshape(1, nocc),
        green_blocks.reshape(nocc, norb),
        scratch=[pltpu.VMEM((1, nocc), jnp.int32), pltpu.VMEM((nocc, norb), bf16), pltpu.SemaphoreType.DMA((2,))],
        ins=HBM,
        grant=PREP,
    )
    pair = call(prep_chol, struct(2, *block.shape), chol_vectors, theta, phase_codes)

    if nchol == 4:
        there = [(0, 2), (2, 3), (3, 1), (1, 0)]
        back = [(b, a) for a, b in there]
        paths = [there, back, [(i, 3 - i) for i in range(4)]]
        first = turn(theta, there)
        early = [first, turn(theta, back)]
        last = turn(theta, [(1, 2), (2, 1)]), turn(first, [(1, 0), (2, 3)])
    else:
        paths = [[(i, (i + d) % nchol) for i in range(nchol)] for d in range(1, nchol)]
        *early, last = [turn(theta, path) for path in paths]
    sources = [list(range(nchol))] + [[a for a, _ in sorted(path, key=lambda p: p[1])] for path in paths]

    paired = swap(pair, 1)
    crossed = swap(chol_vectors, 2)
    relayed = swap(call(functools.partial(relay, padded=padded), block, crossed), 1)
    chol, weight = call(
        functools.partial(place_chol, sources=sources, nocc=nocc, width=width, **sizes),
        (struct(half * LANES, wide), struct(2 * nchol, LANES, dtype=f32)),
        chol_vectors,
        paired,
        crossed,
        relayed,
        phase_codes,
    )
    term = struct(half * LANES, padded, dtype=f32)
    mine = [theta] + early
    theirs = [paired] + [swap(t, 1) for t in early]
    grads, energies = None, []
    for start in range(0, nchol - 1, 3):
        group = mine[start:start + 3] + theirs[start:start + 3]
        walkers = len(group)
        *terms, energy = call(
            functools.partial(first_walkers, first=start, walkers=walkers, nocc=nocc, **sizes),
            (term,) * 4 + (struct(walkers, LANES, dtype=f32),),
            *group,
            chol,
            weight,
            scratch=[pltpu.VMEM((walkers * LANES, wide), bf16), pltpu.VMEM((half * LANES, walkers * LANES), bf16)],
        )
        grads = terms if grads is None else [a + b for a, b in zip(grads, terms)]
        energies += [(energy[:walkers // 2], energy[walkers // 2:])]
    if len(energies) > 1:
        energy = jnp.concatenate([e[i] for i in (0, 1) for e in energies])
    if nchol == 4:
        held = last
        last = call(join, block, *held)

    walkers = 2
    same, other, tmat, theta_s, cotan_s = call(
        functools.partial(last_walkers, nocc=nocc, **sizes),
        (
            struct(half * nocc, padded),
            struct(half * nocc, padded),
            struct(walkers * LANES, half * LANES, dtype=f32),
            struct(walkers * LANES, wide),
            struct(half * LANES, walkers * LANES),
        ),
        last,
        swap(last, 1),
        chol,
        weight,
        grads[2],
        grads[3],
    )
    same, other = swap(same, 2), swap(other, 3)
    tall = max(half, nchol)
    own, core, energy = call(
        functools.partial(chip_walkers, nocc=nocc, rows=rows, **sizes),
        (struct(half, rows, padded, dtype=f32), struct(tall, rows, padded, dtype=f32), struct(nchol, LANES, dtype=f32)),
        tmat,
        theta_s,
        cotan_s,
        grads[0],
        grads[1],
        energy,
    )
    core = swap(core, 1)
    part, *parts = call(
        functools.partial(pick_energies, nocc=nocc), (struct(1, LANES, dtype=f32),) * nchol, energy, core
    )
    parts = [turn(p, [(b, a) for a, b in path]) for p, path in zip(parts, paths)]
    chol_grad, energies = call(
        finish,
        (struct(nocc, gdev, width, dtype=f32), struct(1, 1, dtype=f32)),
        own,
        same,
        other,
        core,
        part,
        *parts,
        out=HBM,
        scratch=[
            pltpu.VMEM((nocc, gdev, width), f32),
            pltpu.VMEM((1, 1), f32),
            pltpu.SemaphoreType.DMA((1 - (-rows // 32),)),
        ],
    )
    return jnp.swapaxes(chol_grad, 0, 1), energies


def solution(mesh):
    placed = (
        P("chol", None, "walk"),
        P(("dom", "walk"), "chol", None, None),
        P(("dom", "walk"), None),
        P(("dom", "walk"), "chol", None),
    )
    return jax.shard_map(
        functools.partial(body, nchol=mesh.shape["chol"], nwalk=mesh.shape["walk"]),
        mesh=mesh,
        in_specs=placed,
        out_specs=(P(("dom", "chol"), None, "walk"), P(("dom", "walk"), "chol")),
        check_vma=False,
    )
```

```python
import functools

import jax
import jax.numpy as jnp
from jax import lax
from jax.experimental import pallas as pl
from jax.experimental.pallas import tpu as pltpu
from jax.sharding import PartitionSpec as P

LANES = 128
SPARE = 92
OPT = {'c1': 'pair', 'a': 8, 'b2': 8, 'force': 0, 'c3': 0, 'hold': 0}
GRANT = 16 * 1024 * 1024
PREP = 56 * 1024 * 1024
HBM = pltpu.MemorySpace.HBM
VMEM = pltpu.MemorySpace.VMEM
bf16, f32 = jnp.bfloat16, jnp.float32


def ceil_to(value, step):
    return -(-value // step) * step


def prep_theta(occ_hbm, green_hbm, out_ref, occ_ref, green_ref, sems, *, width, padded):
    copies = [pltpu.make_async_copy(green_hbm, green_ref, sems.at[0]), pltpu.make_async_copy(occ_hbm, occ_ref, sems.at[1])]
    for copy in copies:
        copy.start()
    out_ref[...] = jnp.zeros_like(out_ref)
    nocc, norb = green_ref.shape
    fold = norb // width // 2
    copies[1].wait()
    pick = (lax.broadcasted_iota(jnp.int32, (nocc, nocc), 0) == occ_ref[...]).astype(bf16)
    copies[0].wait()
    theta = lax.dot_general(pick, green_ref[...], (((0,), (0,)), ((), ())), preferred_element_type=f32)
    for k in range(norb // width):
        row, lane = k // fold * nocc, k % fold * padded
        out_ref[row:row + nocc, lane:lane + width] = theta[:, width * k:width * (k + 1)].astype(bf16)


def prep_chol(chol_ref, code_ref, *refs):
    *theta_ref, pair_ref = refs
    gdev, nocc, width = chol_ref.shape
    half = gdev // 2
    cross_ref = pair_ref
    if theta_ref:
        pair_ref[0] = theta_ref[0][...]
        cross_ref = pair_ref.at[1]
    padded = cross_ref.shape[1] // (half // 2)
    cross_ref[...] = jnp.zeros(cross_ref.shape, bf16)
    fold_half(chol_ref, cross_ref, 1 - lax.rem(lax.axis_index("walk"), 2), padded)
    nchol = code_ref.shape[1]
    shape = (ceil_to(nchol, 8), nchol)
    diagonal = lax.broadcasted_iota(jnp.int32, shape, 0) == lax.broadcasted_iota(jnp.int32, shape, 1)
    codes = jnp.sum(jnp.where(diagonal, code_ref[...], 0).astype(f32), axis=1, keepdims=True)
    lane = cross_ref.shape[1] - padded + width
    cross_ref[:shape[0], lane:lane + 1] = codes.astype(bf16)


def pack(a_ref, b_ref, out_ref):
    out_ref[0] = a_ref[...]
    out_ref[1] = b_ref[...]


def fold_half(chol_ref, out_ref, which, padded):
    gdev, nocc, width = chol_ref.shape
    half = gdev // 2
    for g in range(half):
        row, lane = g // (half // 2) * nocc, g % (half // 2) * padded
        out_ref[row:row + nocc, lane:lane + width] = chol_ref[which * half + g]


def relay(crossed_ref, out_ref, *, padded):
    out_ref[...] = jnp.zeros_like(out_ref)
    fold_half(crossed_ref, out_ref, 1 - lax.rem(lax.axis_index("walk"), 2), padded)


def lift(in_ref, *refs):
    out_ref = refs[-1]
    rows = in_ref.shape[0]
    out_ref[:rows] = in_ref[...]
    out_ref[rows:] = jnp.zeros((out_ref.shape[0] - rows, out_ref.shape[1]), out_ref.dtype)


def source_of(me, path):
    return sum(jnp.where(me == i, s, 0) for i, s in enumerate(path))


def place_chol(
    own_ref, pair_ref, same_ref, other_ref, code_ref, out_ref, weight_ref, *, sources, half, nocc, width, padded
):
    out_ref[...] = jnp.zeros_like(out_ref)
    cross_ref = pair_ref.at[1] if len(pair_ref.shape) == 3 else pair_ref
    h = lax.rem(lax.axis_index("walk"), 2)
    for g in range(half):
        row, lane = g // (half // 2) * nocc, g % (half // 2) * padded
        rows = slice(g * LANES, g * LANES + nocc)
        for s, ref in ((0, own_ref), (2, same_ref)):
            out_ref[rows, column(s, padded)] = jnp.pad(ref[h * half + g], ((0, 0), (0, padded - width)))
        for s, ref in ((1, cross_ref), (3, other_ref)):
            out_ref[rows, column(s, padded)] = ref[row:row + nocc, lane:lane + padded]
    nchol = code_ref.shape[1]
    me = lax.axis_index("chol")
    lane = cross_ref.shape[1] - padded + width
    theirs = cross_ref[:ceil_to(nchol, 16), lane:lane + 1].astype(f32)
    mine = code_ref[...].astype(f32)
    codes = jnp.zeros(weight_ref.shape, f32)
    at = lax.broadcasted_iota(jnp.int32, codes.shape, 0)
    for n, path in enumerate(sources):
        source = source_of(me, path)
        for group, (values, axis) in enumerate(((mine, 1), (theirs, 0))):
            here = lax.broadcasted_iota(jnp.int32, values.shape, axis) == source
            code = jnp.sum(jnp.where(here, values, 0.0), axis=axis, keepdims=True)
            codes = jnp.where(at == group * nchol + n, code, codes)
    weight_ref[...] = -jnp.cos(jnp.pi * codes / 4.0)


def column(s, padded):
    return pl.ds(pl.multiple_of((lax.axis_index("walk") ^ s) * padded, padded), padded)


def place_theta(thetas, theta_s, nocc):
    theta_s[...] = jnp.zeros_like(theta_s)
    for w, (ref, n) in enumerate(thetas):
        theta = ref[n] if len(ref.shape) == 3 else ref[...]
        wide = theta.shape[1]
        for i in range(2):
            theta_s[w * LANES:w * LANES + nocc, i * wide:(i + 1) * wide] = theta[i * nocc:(i + 1) * nocc]


def first_walkers(*refs, first, counts, walkers, half, nocc, padded):
    counts = list(counts)
    *thetas, chol_s, weight_ref, own_ref, core_ref, same_ref, other_ref, energy_ref, theta_s, cotan_s = refs
    place_theta([(ref, n) for ref in thetas for n in range(counts.pop(0))], theta_s, nocc)
    tmat = lax.dot_general(theta_s[...], chol_s[...], (((1,), (1,)), ((), ())), preferred_element_type=f32)
    n = walkers // 2
    for w in range(walkers):
        row = w // n * (weight_ref.shape[0] // 2) + first + w % n
        weight = weight_ref[row:row + 1, :]
        total = jnp.zeros((LANES, LANES), f32)
        for g in range(half):
            block = tmat[w * LANES:(w + 1) * LANES, g * LANES:(g + 1) * LANES]
            total += block * block.T
            cotan_s[g * LANES:(g + 1) * LANES, w * LANES:(w + 1) * LANES] = (weight * block).astype(bf16)
        energy_ref[w:w + 1, :] = -0.5 * jnp.sum(total, axis=0, keepdims=True)
    for s, ref in enumerate((own_ref, core_ref, same_ref, other_ref)):
        ref[...] = jnp.dot(cotan_s[...], theta_s[:, column(s, padded)], preferred_element_type=f32)


def last_walkers(
    mine, theirs, chol_s, weight_ref, same_part, other_part, same_ref, other_ref, tmat_ref, theta_s, cotan_s,
    *, half, nocc, padded
):
    place_theta([(mine, 0), (theirs, 0)], theta_s, nocc)
    tmat = lax.dot_general(theta_s[...], chol_s[...], (((1,), (1,)), ((), ())), preferred_element_type=f32)
    tmat_ref[...] = tmat
    for w in range(2):
        row = (w + 1) * (weight_ref.shape[0] // 2) - 1
        weight = weight_ref[row:row + 1, :]
        for g in range(half):
            block = tmat[w * LANES:(w + 1) * LANES, g * LANES:(g + 1) * LANES]
            cotan_s[g * LANES:(g + 1) * LANES, w * LANES:(w + 1) * LANES] = (weight * block).astype(bf16)
    for ref, part, s in ((same_ref, same_part, 2), (other_ref, other_part, 3)):
        grad = part[...] + jnp.dot(cotan_s[...], theta_s[:, column(s, padded)], preferred_element_type=f32)
        store_grad(grad, ref, half, nocc)


def store_grad(grad, ref, half, nocc):
    for g in range(half):
        if len(ref.shape) == 2:
            ref[g * nocc:(g + 1) * nocc] = grad[g * LANES:g * LANES + nocc, :ref.shape[1]].astype(ref.dtype)
        else:
            ref[g] = grad[g * LANES:g * LANES + ref.shape[1]].astype(ref.dtype)


def chip_walkers(theta_s, cotan_s, own_part, core_part, own_ref, low_ref, high_ref, *, half, nocc, padded):
    for part, s in ((core_part, 1), (own_part, 0)):
        grad = part[...] + jnp.dot(cotan_s[...], theta_s[:, column(s, padded)], preferred_element_type=f32)
        if s == 0:
            store_grad(grad, own_ref, half, nocc)
        else:
            store_grad(grad, low_ref, half // 2, nocc)
            store_grad(grad[half // 2 * LANES:], high_ref, half // 2, nocc)


def last_energies(tmat_ref, first_ref, energy_ref, *, sources, half):
    energy_ref[...] = jnp.zeros_like(energy_ref)
    early = first_ref.shape[0] // 2
    me = lax.axis_index("chol")
    rows = [pl.ds(me ^ source_of(me, path), 1) for path in sources]
    for w in range(2):
        total = jnp.zeros((LANES, LANES), f32)
        for g in range(half):
            block = tmat_ref[w * LANES:(w + 1) * LANES, g * LANES:(g + 1) * LANES]
            total += block * block.T
        for n in range(early):
            energy_ref[w, rows[n], :] = first_ref[w * early + n:w * early + n + 1]
        energy_ref[w, rows[early], :] = -0.5 * jnp.sum(total, axis=0, keepdims=True)


def halve(mine_ref, arrived_ref, keep_ref, send_ref):
    ours, theirs = (ref.at[i] if len(ref.shape) == 3 else ref for i, ref in enumerate((mine_ref, arrived_ref)))
    for n in range(keep_ref.shape[0]):
        for ref, row in ((keep_ref, 2 * n), (send_ref, 2 * n + 1)):
            ref[n:n + 1, :] = ours[row:row + 1, :] + theirs[row:row + 1, :]


def finish(*refs):
    *refs, out_hbm, energy_hbm, out_ref, energy_ref, sems = refs
    own_ref, same_ref, other_ref, low_ref, high_ref, *energy_refs = refs
    half = own_ref.shape[0]
    nocc, gdev, width = out_ref.shape
    h = lax.rem(lax.axis_index("walk"), 2)
    energy = sum(ref[...] for ref in energy_refs)
    energy_ref[...] = jnp.sum(energy, axis=1, keepdims=True)
    copies = [pltpu.make_async_copy(energy_ref, energy_hbm, sems.at[0])]
    copies[0].start()
    for n, start in enumerate(range(0, nocc, 32), start=1):
        stop = min(start + 32, nocc)

        def arrived(*refs):
            n = half // len(refs)
            blocks = [ref[g * nocc + start:g * nocc + stop, :width] for ref in refs for g in range(n)]
            return jnp.stack([block.astype(f32) for block in blocks])

        mine = own_ref[:, start:stop, :width] + arrived(same_ref)
        theirs = arrived(low_ref, high_ref) + arrived(other_ref)
        low = jnp.where(h == 0, mine, theirs)
        high = jnp.where(h == 0, theirs, mine)
        both = jnp.swapaxes(jnp.concatenate([low, high], axis=0), 0, 1)
        out_ref[start:stop] = both
        copies.append(pltpu.make_async_copy(out_ref.at[start:stop], out_hbm.at[start:stop], sems.at[n]))
        copies[-1].start()
    for copy in copies:
        copy.wait()


def call(kernel, outs, *operands, scratch=(), ins=VMEM, out=VMEM, grant=GRANT):
    return pl.pallas_call(
        kernel,
        out_shape=outs,
        in_specs=[pl.BlockSpec(memory_space=ins)] * len(operands),
        out_specs=jax.tree.map(lambda _: pl.BlockSpec(memory_space=out), outs),
        scratch_shapes=scratch,
        compiler_params=pltpu.CompilerParams(vmem_limit_bytes=grant),
    )(*operands)


def body(chol_vectors, green_blocks, phase_codes, occupations, *, nchol, nwalk):
    gdev, nocc, width = chol_vectors.shape
    norb = green_blocks.shape[3]
    half = gdev // 2
    rows = ceil_to(nocc, 8)
    padded = ceil_to(width, LANES)
    wide = padded * nwalk
    sizes = dict(half=half, padded=padded)

    def swap(x, flip):
        return lax.ppermute(x, "walk", [(i, i ^ flip) for i in range(nwalk)])

    def turn(x, pairs):
        return lax.ppermute(x, "chol", pairs)

    def struct(*shape, dtype=bf16):
        return jax.ShapeDtypeStruct(shape, dtype)

    block = struct(2 * nocc, wide // 2)
    theta = call(
        functools.partial(prep_theta, width=width, padded=padded),
        pltpu.VMEM(block.shape, bf16),
        occupations.reshape(1, nocc),
        green_blocks.reshape(nocc, norb),
        scratch=[pltpu.VMEM((1, nocc), jnp.int32), pltpu.VMEM((nocc, norb), bf16), pltpu.SemaphoreType.DMA((2,))],
        ins=HBM,
        grant=PREP,
    )
    if OPT["c1"] == "pair":
        pair = call(prep_chol, struct(2, *block.shape), chol_vectors, phase_codes, theta)
    else:
        pair = call(prep_chol, block, chol_vectors, phase_codes)

    if nchol == 4:
        there = [(0, 2), (2, 3), (3, 1), (1, 0)]
        back = [(b, a) for a, b in there]
        paths = [there, back, [(i, 3 - i) for i in range(4)]]
        first = turn(theta, there)
        early = [first, turn(theta, back)]
        last = turn(first, there)
    else:
        paths = [[(i, (i + d) % nchol) for i in range(nchol)] for d in range(1, nchol)]
        *early, last = [turn(theta, path) for path in paths]
    sources = [list(range(nchol))] + [[a for a, _ in sorted(path, key=lambda p: p[1])] for path in paths]

    paired = swap(pair, 1)
    crossed = swap(chol_vectors, 2)
    relayed = swap(call(functools.partial(relay, padded=padded), block, crossed), 1)
    chol, weight = call(
        functools.partial(place_chol, sources=sources, nocc=nocc, width=width, **sizes),
        (struct(half * LANES, wide), struct(2 * nchol, LANES, dtype=f32)),
        chol_vectors,
        paired,
        crossed,
        relayed,
        phase_codes,
    )
    term = struct(half * LANES, padded, dtype=f32)
    mine = [theta] + early
    def lifted(x, extra, *dummy):
        if not extra:
            return x
        return call(lift, struct(2 * nocc + extra, wide // 2), x, *dummy)

    if OPT["c1"] == "pair":
        a_ops = [paired, swap(lifted(early[0], OPT["a"]), 1)]
        b_dummy = []
    else:
        a_ops = [swap(call(pack, struct(2, *block.shape), theta, early[0]), 1)]
        b_dummy = [paired] if OPT["force"] else []
    theirs = a_ops + [swap(lifted(early[1], OPT["b2"], *b_dummy), 1)] + [swap(t, 1) for t in early[2:]]
    grads, energies = None, []
    for start in range(0, nchol - 1, 3):
        if start == 0 and len(a_ops) == 1:
            group, counts = mine[:3] + theirs[:2], (1, 1, 1, 2, 1)
        else:
            shift = len(a_ops) - 2
            group = mine[start:start + 3] + theirs[start + shift:start + 3 + shift]
            counts = (1,) * len(group)
        walkers = sum(counts)
        *terms, energy = call(
            functools.partial(first_walkers, first=start, counts=counts, walkers=walkers, nocc=nocc, **sizes),
            (term,) * 4 + (struct(walkers, LANES, dtype=f32),),
            *group,
            chol,
            weight,
            scratch=[pltpu.VMEM((walkers * LANES, wide), bf16), pltpu.VMEM((half * LANES, walkers * LANES), bf16)],
        )
        grads = terms if grads is None else [a + b for a, b in zip(grads, terms)]
        energies += [(energy[:walkers // 2], energy[walkers // 2:])]
    if len(energies) > 1:
        energy = jnp.concatenate([e[i] for i in (0, 1) for e in energies])
    theirs_last = swap(lifted(last, OPT["c3"]) if not OPT["hold"] else lax.optimization_barrier((last, energy))[0], 1)

    walkers = 2
    same, other, tmat, theta_s, cotan_s = call(
        functools.partial(last_walkers, nocc=nocc, **sizes),
        (
            struct(half * nocc, padded),
            struct(half * nocc, padded),
            struct(walkers * LANES, half * LANES, dtype=f32),
            struct(walkers * LANES, wide),
            struct(half * LANES, walkers * LANES),
        ),
        last,
        theirs_last,
        chol,
        weight,
        grads[2],
        grads[3],
    )
    same, other = swap(same, 2), swap(other, 3)
    energy = call(
        functools.partial(last_energies, sources=sources, half=half),
        struct(2, nchol + SPARE, LANES, dtype=f32),
        tmat,
        energy,
    )
    own, *core = call(
        functools.partial(chip_walkers, nocc=nocc, **sizes),
        (struct(half, rows, padded, dtype=f32),) + (struct(half // 2 * nocc, width),) * 2,
        theta_s,
        cotan_s,
        grads[0],
        grads[1],
    )
    core = [swap(c, 1) for c in core]
    arrived, n, flip = swap(energy, 1), nchol // 2, 1
    while n:
        energy, send = call(halve, (struct(n, LANES, dtype=f32),) * 2, energy, arrived)
        arrived = turn(send, [(i, i ^ flip) for i in range(nchol)])
        n, flip = n // 2, flip * 2
    chol_grad, energies = call(
        finish,
        (struct(nocc, gdev, width, dtype=f32), struct(1, 1, dtype=f32)),
        own,
        same,
        other,
        *core,
        energy,
        arrived,
        out=HBM,
        scratch=[
            pltpu.VMEM((nocc, gdev, width), f32),
            pltpu.VMEM((1, 1), f32),
            pltpu.SemaphoreType.DMA((1 - (-rows // 32),)),
        ],
    )
    return jnp.swapaxes(chol_grad, 0, 1), energies


def solution(mesh):
    placed = (
        P("chol", None, "walk"),
        P(("dom", "walk"), "chol", None, None),
        P(("dom", "walk"), None),
        P(("dom", "walk"), "chol", None),
    )
    return jax.shard_map(
        functools.partial(body, nchol=mesh.shape["chol"], nwalk=mesh.shape["walk"]),
        mesh=mesh,
        in_specs=placed,
        out_specs=(P(("dom", "chol"), None, "walk"), P(("dom", "walk"), "chol")),
        check_vma=False,
    )
```

```python
import functools

import jax
import jax.numpy as jnp
from jax import lax
from jax.experimental import pallas as pl
from jax.experimental.pallas import tpu as pltpu
from jax.sharding import PartitionSpec as P

LANES = 128
STEP = 32
HELD = 1
SPARE = 104
OPT = {'aw': 1, 'bw': 1, 'ar': 2, 'br': 4, 'rel': 0, 'hold': 1, 'c1r': 0}
GRANT = 16 * 1024 * 1024
PREP = 56 * 1024 * 1024
HBM = pltpu.MemorySpace.HBM
VMEM = pltpu.MemorySpace.VMEM
bf16, f32 = jnp.bfloat16, jnp.float32


def ceil_to(value, step):
    return -(-value // step) * step


def prep_theta(occ_hbm, green_hbm, chol_hbm, out_ref, chol_ref, occ_ref, green_ref, sems, *, width, padded):
    pairs = (green_hbm, green_ref), (occ_hbm, occ_ref), (chol_hbm, chol_ref)
    copies = [pltpu.make_async_copy(source, target, sems.at[i]) for i, (source, target) in enumerate(pairs)]
    for copy in copies:
        copy.start()
    out_ref[...] = jnp.zeros_like(out_ref)
    nocc, norb = green_ref.shape
    fold = norb // width // 2
    copies[1].wait()
    pick = (lax.broadcasted_iota(jnp.int32, (nocc, nocc), 0) == occ_ref[...]).astype(bf16)
    copies[0].wait()
    theta = lax.dot_general(pick, green_ref[...], (((0,), (0,)), ((), ())), preferred_element_type=f32)
    for k in range(norb // width):
        row, lane = k // fold * nocc, k % fold * padded
        out_ref[row:row + nocc, lane:lane + width] = theta[:, width * k:width * (k + 1)].astype(bf16)
    copies[2].wait()


def prep_chol(chol_ref, code_ref, cross_ref):
    gdev, nocc, width = chol_ref.shape
    padded = cross_ref.shape[1] // (gdev // 4)
    cross_ref[...] = jnp.zeros(cross_ref.shape, bf16)
    fold_half(chol_ref, cross_ref, 1 - lax.rem(lax.axis_index("walk"), 2), padded)
    nchol = code_ref.shape[1]
    shape = (ceil_to(nchol, 8), nchol)
    diagonal = lax.broadcasted_iota(jnp.int32, shape, 0) == lax.broadcasted_iota(jnp.int32, shape, 1)
    codes = jnp.sum(jnp.where(diagonal, code_ref[...], 0).astype(f32), axis=1, keepdims=True)
    lane = cross_ref.shape[1] - padded + width
    cross_ref[:shape[0], lane:lane + 1] = codes.astype(bf16)


def mail(*refs, width):
    *ins, out_ref = refs
    out_ref[...] = jnp.zeros_like(out_ref)
    for n, ref in enumerate(ins):
        rows, padded = ref.shape[0], ref.shape[1] // 2
        target = out_ref.at[n] if len(out_ref.shape) == 3 else out_ref
        span = target.shape[1] // 2
        for k in range(2):
            target[:rows, k * span:k * span + width] = ref[:, k * padded:k * padded + width]


def fold_half(chol_ref, out_ref, which, padded):
    gdev, nocc, width = chol_ref.shape
    half = gdev // 2
    for g in range(half):
        row, lane = g // (half // 2) * nocc, g % (half // 2) * padded
        out_ref[row:row + nocc, lane:lane + width] = chol_ref[which * half + g]


def relay(crossed_ref, out_ref):
    half = crossed_ref.shape[0] // 2
    h = lax.rem(lax.axis_index("walk"), 2)
    for g in range(half):
        out_ref[g] = crossed_ref[(1 - h) * half + g]


def source_of(me, path):
    return sum(jnp.where(me == i, s, 0) for i, s in enumerate(path))


def place_chol(
    own_ref, cross_ref, same_ref, other_ref, code_ref, out_ref, weight_ref, *, sources, half, nocc, width, padded
):
    out_ref[...] = jnp.zeros_like(out_ref)
    h = lax.rem(lax.axis_index("walk"), 2)
    for g in range(half):
        row, lane = g // (half // 2) * nocc, g % (half // 2) * padded
        rows = slice(g * LANES, g * LANES + nocc)
        for s, block in ((0, own_ref[h * half + g]), (2, same_ref[h * half + g]), (3, other_ref[g])):
            out_ref[rows, column(s, padded)] = jnp.pad(block, ((0, 0), (0, padded - width)))
        out_ref[rows, column(1, padded)] = cross_ref[row:row + nocc, lane:lane + padded]
    nchol = code_ref.shape[1]
    me = lax.axis_index("chol")
    lane = cross_ref.shape[1] - padded + width
    theirs = cross_ref[:ceil_to(nchol, 16), lane:lane + 1].astype(f32)
    mine = code_ref[...].astype(f32)
    codes = jnp.zeros(weight_ref.shape, f32)
    at = lax.broadcasted_iota(jnp.int32, codes.shape, 0)
    for n, path in enumerate(sources):
        source = source_of(me, path)
        for group, (values, axis) in enumerate(((mine, 1), (theirs, 0))):
            here = lax.broadcasted_iota(jnp.int32, values.shape, axis) == source
            code = jnp.sum(jnp.where(here, values, 0.0), axis=axis, keepdims=True)
            codes = jnp.where(at == group * nchol + n, code, codes)
    weight_ref[...] = -jnp.cos(jnp.pi * codes / 4.0)


def column(s, padded):
    return pl.ds(pl.multiple_of((lax.axis_index("walk") ^ s) * padded, padded), padded)


def place_theta(thetas, theta_s, nocc, width, padded):
    theta_s[...] = jnp.zeros_like(theta_s)
    for w, (ref, n) in enumerate(thetas):
        theta = ref[n] if len(ref.shape) == 3 else ref[...]
        span = theta.shape[1] // 2
        rows = slice(w * LANES, w * LANES + nocc)
        for i in range(2):
            part = theta[i * nocc:(i + 1) * nocc]
            if span == padded:
                theta_s[rows, 2 * i * padded:2 * (i + 1) * padded] = part
            else:
                for k in range(2):
                    lane = (2 * i + k) * padded
                    theta_s[rows, lane:lane + width] = part[:, k * span:k * span + width]


def first_walkers(*refs, first, counts, walkers, half, nocc, width, padded):
    counts = list(counts)
    *thetas, chol_s, weight_ref, same_ref, other_ref, tmat_ref, theta_s, cotan_s = refs
    place_theta([(ref, n) for ref in thetas for n in range(counts.pop(0))], theta_s, nocc, width, padded)
    tmat = lax.dot_general(theta_s[...], chol_s[...], (((1,), (1,)), ((), ())), preferred_element_type=f32)
    tmat_ref[...] = tmat
    n = walkers // 2
    for w in range(walkers):
        row = w // n * (weight_ref.shape[0] // 2) + first + w % n
        weight = weight_ref[row:row + 1, :]
        for g in range(half):
            block = tmat[w * LANES:(w + 1) * LANES, g * LANES:(g + 1) * LANES]
            cotan_s[g * LANES:(g + 1) * LANES, w * LANES:(w + 1) * LANES] = (weight * block).astype(bf16)
    for s, ref in ((2, same_ref), (3, other_ref)):
        ref[...] = jnp.dot(cotan_s[...], theta_s[:, column(s, padded)], preferred_element_type=f32)


def first_energies(tmat_ref, energy_ref, *, half):
    for w in range(energy_ref.shape[0]):
        total = jnp.zeros((LANES, LANES), f32)
        for g in range(half):
            block = tmat_ref[w * LANES:(w + 1) * LANES, g * LANES:(g + 1) * LANES]
            total += block * block.T
        energy_ref[w:w + 1, :] = -0.5 * jnp.sum(total, axis=0, keepdims=True)


def last_walkers(
    mine, theirs, chol_s, weight_ref, same_part, other_part, first_ref, same_ref, other_ref, energy_ref, theta_s, cotan_s,
    *, sources, half, nocc, width, padded
):
    place_theta([(mine, 0), (theirs, 0)], theta_s, nocc, width, padded)
    tmat = lax.dot_general(theta_s[...], chol_s[...], (((1,), (1,)), ((), ())), preferred_element_type=f32)
    for w in range(2):
        row = (w + 1) * (weight_ref.shape[0] // 2) - 1
        weight = weight_ref[row:row + 1, :]
        for g in range(half):
            block = tmat[w * LANES:(w + 1) * LANES, g * LANES:(g + 1) * LANES]
            cotan_s[g * LANES:(g + 1) * LANES, w * LANES:(w + 1) * LANES] = (weight * block).astype(bf16)
    for ref, part, s in ((same_ref, same_part, 2), (other_ref, other_part, 3)):
        grad = part[...] + jnp.dot(cotan_s[...], theta_s[:, column(s, padded)], preferred_element_type=f32)
        store_grad(grad, ref, half, nocc)
    energy_ref[...] = jnp.zeros_like(energy_ref)
    early = first_ref.shape[0] // 2
    me = lax.axis_index("chol")
    rows = [pl.ds(me ^ source_of(me, path), 1) for path in sources]
    for w in range(2):
        total = jnp.zeros((LANES, LANES), f32)
        for g in range(half):
            block = tmat[w * LANES:(w + 1) * LANES, g * LANES:(g + 1) * LANES]
            total += block * block.T
        for n in range(early):
            energy_ref[w, rows[n], :] = first_ref[w * early + n:w * early + n + 1]
        energy_ref[w, rows[early], :] = -0.5 * jnp.sum(total, axis=0, keepdims=True)


def store_grad(grad, ref, half, nocc):
    for g in range(half):
        if len(ref.shape) == 2:
            ref[g * nocc:(g + 1) * nocc] = grad[g * LANES:g * LANES + nocc, :ref.shape[1]].astype(ref.dtype)
        else:
            ref[g] = grad[g * LANES:g * LANES + ref.shape[1]].astype(ref.dtype)


def chip_walkers(*refs, half, nocc, padded):
    *factors, own_ref, low_ref, high_ref = refs
    for s in (1, 0):
        grad = 0.0
        for cotan_s, theta_s in zip(factors[::2], factors[1::2]):
            grad += jnp.dot(cotan_s[...], theta_s[:, column(s, padded)], preferred_element_type=f32)
        if s == 0:
            store_grad(grad, own_ref, half, nocc)
        else:
            store_grad(grad, low_ref, half // 2, nocc)
            store_grad(grad[half // 2 * LANES:], high_ref, half // 2, nocc)


def halve(mine_ref, arrived_ref, keep_ref, send_ref):
    ours, theirs = (ref.at[i] if len(ref.shape) == 3 else ref for i, ref in enumerate((mine_ref, arrived_ref)))
    for n in range(keep_ref.shape[0]):
        for ref, row in ((keep_ref, 2 * n), (send_ref, 2 * n + 1)):
            ref[n:n + 1, :] = ours[row:row + 1, :] + theirs[row:row + 1, :]


def finish(*refs):
    *refs, out_hbm, energy_hbm, out_ref, energy_ref, sems = refs
    own_ref, same_ref, other_ref, low_ref, high_ref, *energy_refs = refs
    half = own_ref.shape[0]
    nocc, gdev, width = out_ref.shape
    h = lax.rem(lax.axis_index("walk"), 2)
    energy = sum(ref[...] for ref in energy_refs)
    energy_ref[...] = jnp.sum(energy, axis=1, keepdims=True)
    copies = [pltpu.make_async_copy(energy_ref, energy_hbm, sems.at[0])]
    copies[0].start()

    def arrived(*refs):
        n = half // len(refs)
        blocks = [ref[g * nocc + start:g * nocc + stop, :width] for ref in refs for g in range(n)]
        return jnp.stack([block.astype(f32) for block in blocks])

    for n, start in enumerate(range(0, nocc, STEP), start=1):
        stop = min(start + STEP, nocc)
        mine = own_ref[:, start:stop, :width] + arrived(same_ref)
        theirs = arrived(low_ref, high_ref) + arrived(other_ref)

        @pl.when(h == 0)
        def _():
            out_ref[start:stop] = jnp.swapaxes(jnp.concatenate([mine, theirs], axis=0), 0, 1)

        @pl.when(h == 1)
        def _():
            out_ref[start:stop] = jnp.swapaxes(jnp.concatenate([theirs, mine], axis=0), 0, 1)

        copies.append(pltpu.make_async_copy(out_ref.at[start:stop], out_hbm.at[start:stop], sems.at[n]))
        copies[-1].start()
    for copy in copies:
        copy.wait()


def call(kernel, outs, *operands, scratch=(), ins=VMEM, out=VMEM, grant=GRANT):
    return pl.pallas_call(
        kernel,
        out_shape=outs,
        in_specs=[pl.BlockSpec(memory_space=ins)] * len(operands),
        out_specs=jax.tree.map(lambda _: pl.BlockSpec(memory_space=out), outs),
        scratch_shapes=scratch,
        compiler_params=pltpu.CompilerParams(vmem_limit_bytes=grant),
    )(*operands)


def body(chol_vectors, green_blocks, phase_codes, occupations, *, nchol, nwalk):
    gdev, nocc, width = chol_vectors.shape
    norb = green_blocks.shape[3]
    half = gdev // 2
    rows = ceil_to(nocc, 8)
    padded = ceil_to(width, LANES)
    wide = padded * nwalk
    sizes = dict(half=half, padded=padded)

    def swap(x, flip):
        return lax.ppermute(x, "walk", [(i, i ^ flip) for i in range(nwalk)])

    def turn(x, pairs):
        return lax.ppermute(x, "chol", pairs)

    def struct(*shape, dtype=bf16):
        return jax.ShapeDtypeStruct(shape, dtype)

    block = struct(2 * nocc, wide // 2)
    theta, chol_vectors = call(
        functools.partial(prep_theta, width=width, padded=padded),
        (pltpu.VMEM(block.shape, bf16), pltpu.VMEM((nocc, gdev, width), bf16)),
        occupations.reshape(1, nocc),
        green_blocks.reshape(nocc, norb),
        jnp.swapaxes(chol_vectors, 0, 1),
        scratch=[pltpu.VMEM((1, nocc), jnp.int32), pltpu.VMEM((nocc, norb), bf16), pltpu.SemaphoreType.DMA((3,))],
        ins=HBM,
        grant=PREP,
    )
    chol_vectors = jnp.swapaxes(chol_vectors, 0, 1)
    cross = call(prep_chol, struct(2 * nocc + OPT["c1r"], wide // 2), chol_vectors, phase_codes)

    if nchol == 4:
        there = [(0, 2), (2, 3), (3, 1), (1, 0)]
        back = [(b, a) for a, b in there]
        paths = [there, back, [(i, 3 - i) for i in range(4)]]
        first = turn(theta, there)
        early = [first, turn(theta, back)]
        last = turn(first, there)
    else:
        paths = [[(i, (i + d) % nchol) for i in range(nchol)] for d in range(1, nchol)]
        *early, last = [turn(theta, path) for path in paths]
    sources = [list(range(nchol))] + [[a for a, _ in sorted(path, key=lambda p: p[1])] for path in paths]

    paired = swap(cross, 1)
    crossed = swap(chol_vectors, 2)
    relayed = swap(call(relay, struct(half, nocc + OPT["rel"], width), crossed), 1)
    chol, weight = call(
        functools.partial(place_chol, sources=sources, nocc=nocc, width=width, **sizes),
        (struct(half * LANES, wide), struct(2 * nchol, LANES, dtype=f32)),
        chol_vectors,
        paired,
        crossed,
        relayed,
        phase_codes,
    )
    term = struct(half * LANES, padded, dtype=f32)
    mine = [theta] + early
    def message(extra, span, *blocks):
        shape = (2 * nocc + extra, 2 * span)
        return call(
            functools.partial(mail, width=width), struct(*shape) if len(blocks) == 1 else struct(2, *shape), *blocks
        )

    a_ops = [swap(message(OPT["ar"], width if OPT["aw"] else padded, theta, early[0]), 1)]
    b_op = message(OPT["br"], width if OPT["bw"] else padded, early[1])
    theirs = a_ops + [swap(b_op, 1)] + [swap(t, 1) for t in early[2:]]
    grads, energies, factors = None, [], []
    for start in range(0, nchol - 1, 3):
        if start == 0 and len(a_ops) == 1:
            group, counts = mine[:3] + theirs[:2], (1, 1, 1, 2, 1)
        else:
            shift = len(a_ops) - 2
            group = mine[start:start + 3] + theirs[start + shift:start + 3 + shift]
            counts = (1,) * len(group)
        walkers = sum(counts)
        *terms, tmat, theta_s, cotan_s = call(
            functools.partial(
                first_walkers, first=start, counts=counts, walkers=walkers, nocc=nocc, width=width, **sizes
            ),
            (
                term,
                term,
                struct(walkers * LANES, half * LANES, dtype=f32),
                struct(walkers * LANES, wide),
                struct(half * LANES, walkers * LANES),
            ),
            *group,
            chol,
            weight,
        )
        energy = call(functools.partial(first_energies, half=half), struct(walkers, LANES, dtype=f32), tmat)
        grads = terms if grads is None else [a + b for a, b in zip(grads, terms)]
        energies += [(energy[:walkers // 2], energy[walkers // 2:])]
        factors += [cotan_s, theta_s]
    if len(energies) > 1:
        energy = jnp.concatenate([e[i] for i in (0, 1) for e in energies])
    theirs_last = swap(lax.optimization_barrier((last, grads[0]))[0], 1)

    walkers = 2
    same, other, energy, theta_s, cotan_s = call(
        functools.partial(last_walkers, sources=sources, nocc=nocc, width=width, **sizes),
        (
            struct(half * nocc, padded),
            struct(half * nocc, padded),
            struct(2, nchol + SPARE, LANES, dtype=f32),
            struct(walkers * LANES, wide),
            struct(half * LANES, walkers * LANES),
        ),
        last,
        theirs_last,
        chol,
        weight,
        grads[0],
        grads[1],
        energy,
    )
    same, other = swap(same, 2), swap(other, 3)
    arrived, n, flip = swap(energy, 1), nchol // 2, 1
    while n:
        energy, send = call(halve, (struct(n, LANES, dtype=f32),) * 2, energy, arrived)
        arrived = turn(send, [(i, i ^ flip) for i in range(nchol)])
        if flip == HELD:
            theta_s, _ = lax.optimization_barrier((theta_s, arrived))
        n, flip = n // 2, flip * 2
    own, *core = call(
        functools.partial(chip_walkers, nocc=nocc, **sizes),
        (struct(half, rows, padded, dtype=f32),) + (struct(half // 2 * nocc, width),) * 2,
        *factors,
        cotan_s,
        theta_s,
    )
    core = [swap(c, 1) for c in core]
    chol_grad, energies = call(
        finish,
        (struct(nocc, gdev, width, dtype=f32), struct(1, 1, dtype=f32)),
        own,
        same,
        other,
        *core,
        energy,
        arrived,
        out=HBM,
        scratch=[
            pltpu.VMEM((nocc, gdev, width), f32),
            pltpu.VMEM((1, 1), f32),
            pltpu.SemaphoreType.DMA((1 - (-nocc // STEP),)),
        ],
    )
    return jnp.swapaxes(chol_grad, 0, 1), energies


def solution(mesh):
    placed = (
        P("chol", None, "walk"),
        P(("dom", "walk"), "chol", None, None),
        P(("dom", "walk"), None),
        P(("dom", "walk"), "chol", None),
    )
    return jax.shard_map(
        functools.partial(body, nchol=mesh.shape["chol"], nwalk=mesh.shape["walk"]),
        mesh=mesh,
        in_specs=placed,
        out_specs=(P(("dom", "chol"), None, "walk"), P(("dom", "walk"), "chol")),
        check_vma=False,
    )
```

```python
import functools

import jax
import jax.numpy as jnp
from jax import lax
from jax.experimental import pallas as pl
from jax.experimental.pallas import tpu as pltpu
from jax.sharding import PartitionSpec as P

LANES = 128
STEP = 32
HELD = 1
SPARE = 104
OPT = {'aw': 1, 'bw': 1, 'ar': 2, 'br': 4, 'rel': 0, 'hold': 1, 'c1r': 0}
GRANT = 16 * 1024 * 1024
PREP = 56 * 1024 * 1024
HBM = pltpu.MemorySpace.HBM
VMEM = pltpu.MemorySpace.VMEM
bf16, f32 = jnp.bfloat16, jnp.float32


def ceil_to(value, step):
    return -(-value // step) * step


def prep_theta(occ_hbm, green_hbm, chol_hbm, out_ref, chol_ref, occ_ref, green_ref, sems, *, width, padded):
    pairs = (green_hbm, green_ref), (occ_hbm, occ_ref), (chol_hbm, chol_ref)
    copies = [pltpu.make_async_copy(source, target, sems.at[i]) for i, (source, target) in enumerate(pairs)]
    for copy in copies:
        copy.start()
    out_ref[...] = jnp.zeros_like(out_ref)
    nocc, norb = green_ref.shape
    fold = norb // width // 2
    copies[1].wait()
    row, lane = (lax.broadcasted_iota(jnp.int32, (nocc, nocc), axis) for axis in (0, 1))
    source = jnp.sum(jnp.where(row == lane, occ_ref[...], 0).astype(f32), axis=1, keepdims=True)
    pick = (source == lane.astype(f32)).astype(bf16)
    copies[0].wait()
    theta = jnp.dot(pick, green_ref[...], preferred_element_type=f32)
    for k in range(norb // width):
        row, lane = k // fold * nocc, k % fold * padded
        out_ref[row:row + nocc, lane:lane + width] = theta[:, width * k:width * (k + 1)].astype(bf16)
    copies[2].wait()


def prep_chol(chol_ref, code_ref, cross_ref):
    gdev, nocc, width = chol_ref.shape
    half = gdev // 2
    h = lax.rem(lax.axis_index("walk"), 2)
    for g in range(half):
        row, lane = g // (half // 2) * nocc, g % (half // 2) * width
        cross_ref[row:row + nocc, lane:lane + width] = chol_ref[(1 - h) * half + g]
    cross_ref[2 * nocc:, :] = jnp.zeros((1, cross_ref.shape[1]), bf16)
    cross_ref[2 * nocc:, :code_ref.shape[1]] = code_ref[...].astype(f32).astype(bf16)


def mail(*refs, width):
    *ins, out_ref = refs
    out_ref[...] = jnp.zeros_like(out_ref)
    for n, ref in enumerate(ins):
        rows, padded = ref.shape[0], ref.shape[1] // 2
        target = out_ref.at[n] if len(out_ref.shape) == 3 else out_ref
        span = target.shape[1] // 2
        for k in range(2):
            target[:rows, k * span:k * span + width] = ref[:, k * padded:k * padded + width]


def relay(crossed_ref, out_ref):
    half = crossed_ref.shape[0] // 2
    h = lax.rem(lax.axis_index("walk"), 2)
    for g in range(half):
        out_ref[g] = crossed_ref[(1 - h) * half + g]


def source_of(me, path):
    return sum(jnp.where(me == i, s, 0) for i, s in enumerate(path))


def place_chol(
    own_ref, cross_ref, same_ref, other_ref, code_ref, out_ref, weight_ref, *, sources, half, nocc, width, padded
):
    out_ref[...] = jnp.zeros_like(out_ref)
    h = lax.rem(lax.axis_index("walk"), 2)
    for g in range(half):
        row, lane = g // (half // 2) * nocc, g % (half // 2) * width
        rows = slice(g * LANES, g * LANES + nocc)
        crossed = cross_ref[row:row + nocc, lane:lane + width]
        for s, block in enumerate((own_ref[h * half + g], crossed, same_ref[h * half + g], other_ref[g])):
            out_ref[rows, column(s, padded)] = jnp.pad(block, ((0, 0), (0, padded - width)))
    nchol = code_ref.shape[1]
    me = lax.axis_index("chol")
    mine = code_ref[...].astype(f32)
    theirs = cross_ref[2 * nocc:, :nchol].astype(f32)
    codes = jnp.zeros(weight_ref.shape, f32)
    at = lax.broadcasted_iota(jnp.int32, codes.shape, 0)
    for n, path in enumerate(sources):
        source = source_of(me, path)
        for group, values in enumerate((mine, theirs)):
            here = lax.broadcasted_iota(jnp.int32, values.shape, 1) == source
            code = jnp.sum(jnp.where(here, values, 0.0), axis=1, keepdims=True)
            codes = jnp.where(at == group * nchol + n, code, codes)
    weight_ref[...] = -jnp.cos(jnp.pi * codes / 4.0)


def column(s, padded):
    return pl.ds(pl.multiple_of((lax.axis_index("walk") ^ s) * padded, padded), padded)


def place_theta(thetas, theta_s, nocc, width, padded):
    theta_s[...] = jnp.zeros_like(theta_s)
    for w, (ref, n) in enumerate(thetas):
        theta = ref[n] if len(ref.shape) == 3 else ref[...]
        span = theta.shape[1] // 2
        rows = slice(w * LANES, w * LANES + nocc)
        for i in range(2):
            part = theta[i * nocc:(i + 1) * nocc]
            if span == padded:
                theta_s[rows, 2 * i * padded:2 * (i + 1) * padded] = part
            else:
                for k in range(2):
                    lane = (2 * i + k) * padded
                    theta_s[rows, lane:lane + width] = part[:, k * span:k * span + width]


def first_walkers(*refs, first, counts, walkers, half, nocc, width, padded):
    counts = list(counts)
    *thetas, chol_s, weight_ref, same_ref, other_ref, tmat_ref, theta_s, cotan_s = refs
    place_theta([(ref, n) for ref in thetas for n in range(counts.pop(0))], theta_s, nocc, width, padded)
    tmat = lax.dot_general(theta_s[...], chol_s[...], (((1,), (1,)), ((), ())), preferred_element_type=f32)
    tmat_ref[...] = tmat
    n = walkers // 2
    for w in range(walkers):
        row = w // n * (weight_ref.shape[0] // 2) + first + w % n
        weight = weight_ref[row:row + 1, :]
        for g in range(half):
            block = tmat[w * LANES:(w + 1) * LANES, g * LANES:(g + 1) * LANES]
            cotan_s[g * LANES:(g + 1) * LANES, w * LANES:(w + 1) * LANES] = (weight * block).astype(bf16)
    for s, ref in ((2, same_ref), (3, other_ref)):
        ref[...] = jnp.dot(cotan_s[...], theta_s[:, column(s, padded)], preferred_element_type=f32)


def first_energies(tmat_ref, energy_ref, *, half):
    for w in range(energy_ref.shape[0]):
        total = jnp.zeros((LANES, LANES), f32)
        for g in range(half):
            block = tmat_ref[w * LANES:(w + 1) * LANES, g * LANES:(g + 1) * LANES]
            total += block * block.T
        energy_ref[w:w + 1, :] = -0.5 * jnp.sum(total, axis=0, keepdims=True)


def last_walkers(
    mine, theirs, chol_s, weight_ref, same_part, other_part, first_ref, same_ref, other_ref, energy_ref, theta_s, cotan_s,
    *, sources, half, nocc, width, padded
):
    place_theta([(mine, 0), (theirs, 0)], theta_s, nocc, width, padded)
    tmat = lax.dot_general(theta_s[...], chol_s[...], (((1,), (1,)), ((), ())), preferred_element_type=f32)
    for w in range(2):
        row = (w + 1) * (weight_ref.shape[0] // 2) - 1
        weight = weight_ref[row:row + 1, :]
        for g in range(half):
            block = tmat[w * LANES:(w + 1) * LANES, g * LANES:(g + 1) * LANES]
            cotan_s[g * LANES:(g + 1) * LANES, w * LANES:(w + 1) * LANES] = (weight * block).astype(bf16)
    for ref, part, s in ((same_ref, same_part, 2), (other_ref, other_part, 3)):
        grad = part[...] + jnp.dot(cotan_s[...], theta_s[:, column(s, padded)], preferred_element_type=f32)
        store_grad(grad, ref, half, nocc)
    energy_ref[...] = jnp.zeros_like(energy_ref)
    early = first_ref.shape[0] // 2
    me = lax.axis_index("chol")
    rows = [pl.ds(me ^ source_of(me, path), 1) for path in sources]
    for w in range(2):
        total = jnp.zeros((LANES, LANES), f32)
        for g in range(half):
            block = tmat[w * LANES:(w + 1) * LANES, g * LANES:(g + 1) * LANES]
            total += block * block.T
        for n in range(early):
            energy_ref[w, rows[n], :] = first_ref[w * early + n:w * early + n + 1]
        energy_ref[w, rows[early], :] = -0.5 * jnp.sum(total, axis=0, keepdims=True)


def store_grad(grad, ref, half, nocc):
    for g in range(half):
        if len(ref.shape) == 2:
            ref[g * nocc:(g + 1) * nocc] = grad[g * LANES:g * LANES + nocc, :ref.shape[1]].astype(ref.dtype)
        else:
            ref[g] = grad[g * LANES:g * LANES + ref.shape[1]].astype(ref.dtype)


def chip_walkers(*refs, half, nocc, padded):
    *factors, own_ref, low_ref, high_ref = refs
    for s in (1, 0):
        grad = 0.0
        for cotan_s, theta_s in zip(factors[::2], factors[1::2]):
            grad += jnp.dot(cotan_s[...], theta_s[:, column(s, padded)], preferred_element_type=f32)
        if s == 0:
            store_grad(grad, own_ref, half, nocc)
        else:
            store_grad(grad, low_ref, half // 2, nocc)
            store_grad(grad[half // 2 * LANES:], high_ref, half // 2, nocc)


def halve(mine_ref, arrived_ref, keep_ref, send_ref):
    ours, theirs = (ref.at[i] if len(ref.shape) == 3 else ref for i, ref in enumerate((mine_ref, arrived_ref)))
    for n in range(keep_ref.shape[0]):
        for ref, row in ((keep_ref, 2 * n), (send_ref, 2 * n + 1)):
            ref[n:n + 1, :] = ours[row:row + 1, :] + theirs[row:row + 1, :]


def finish(*refs):
    *refs, out_hbm, energy_hbm, out_ref, energy_ref, sems = refs
    own_ref, same_ref, other_ref, low_ref, high_ref, *energy_refs = refs
    half = own_ref.shape[0]
    nocc, gdev, width = out_ref.shape
    h = lax.rem(lax.axis_index("walk"), 2)
    energy = sum(ref[...] for ref in energy_refs)
    energy_ref[...] = jnp.sum(energy, axis=1, keepdims=True)
    copies = [pltpu.make_async_copy(energy_ref, energy_hbm, sems.at[0])]
    copies[0].start()

    def arrived(*refs):
        n = half // len(refs)
        blocks = [ref[g * nocc + start:g * nocc + stop, :width] for ref in refs for g in range(n)]
        return jnp.stack([block.astype(f32) for block in blocks])

    for n, start in enumerate(range(0, nocc, STEP), start=1):
        stop = min(start + STEP, nocc)
        mine = own_ref[:, start:stop, :width] + arrived(same_ref)
        theirs = arrived(low_ref, high_ref) + arrived(other_ref)

        @pl.when(h == 0)
        def _():
            out_ref[start:stop] = jnp.swapaxes(jnp.concatenate([mine, theirs], axis=0), 0, 1)

        @pl.when(h == 1)
        def _():
            out_ref[start:stop] = jnp.swapaxes(jnp.concatenate([theirs, mine], axis=0), 0, 1)

        copies.append(pltpu.make_async_copy(out_ref.at[start:stop], out_hbm.at[start:stop], sems.at[n]))
        copies[-1].start()
    for copy in copies:
        copy.wait()


def call(kernel, outs, *operands, scratch=(), ins=VMEM, out=VMEM, grant=GRANT):
    return pl.pallas_call(
        kernel,
        out_shape=outs,
        in_specs=[pl.BlockSpec(memory_space=ins)] * len(operands),
        out_specs=jax.tree.map(lambda _: pl.BlockSpec(memory_space=out), outs),
        scratch_shapes=scratch,
        compiler_params=pltpu.CompilerParams(vmem_limit_bytes=grant),
    )(*operands)


def body(chol_vectors, green_blocks, phase_codes, occupations, *, nchol, nwalk):
    gdev, nocc, width = chol_vectors.shape
    norb = green_blocks.shape[3]
    half = gdev // 2
    rows = ceil_to(nocc, 8)
    padded = ceil_to(width, LANES)
    wide = padded * nwalk
    sizes = dict(half=half, padded=padded)

    def swap(x, flip):
        return lax.ppermute(x, "walk", [(i, i ^ flip) for i in range(nwalk)])

    def turn(x, pairs):
        return lax.ppermute(x, "chol", pairs)

    def struct(*shape, dtype=bf16):
        return jax.ShapeDtypeStruct(shape, dtype)

    block = struct(2 * nocc, wide // 2)
    theta, chol_vectors = call(
        functools.partial(prep_theta, width=width, padded=padded),
        (pltpu.VMEM(block.shape, bf16), pltpu.VMEM((nocc, gdev, width), bf16)),
        occupations.reshape(1, nocc),
        green_blocks.reshape(nocc, norb),
        jnp.swapaxes(chol_vectors, 0, 1),
        scratch=[pltpu.VMEM((1, nocc), jnp.int32), pltpu.VMEM((nocc, norb), bf16), pltpu.SemaphoreType.DMA((3,))],
        ins=HBM,
        grant=PREP,
    )
    chol_vectors = jnp.swapaxes(chol_vectors, 0, 1)
    cross = call(prep_chol, struct(2 * nocc + 1, half // 2 * width), chol_vectors, phase_codes)

    if nchol == 4:
        there = [(0, 2), (2, 3), (3, 1), (1, 0)]
        back = [(b, a) for a, b in there]
        paths = [there, back, [(i, 3 - i) for i in range(4)]]
        first = turn(theta, there)
        early = [first, turn(theta, back)]
        last = turn(first, there)
    else:
        paths = [[(i, (i + d) % nchol) for i in range(nchol)] for d in range(1, nchol)]
        *early, last = [turn(theta, path) for path in paths]
    sources = [list(range(nchol))] + [[a for a, _ in sorted(path, key=lambda p: p[1])] for path in paths]

    paired = swap(cross, 1)
    crossed = swap(chol_vectors, 2)
    relayed = swap(call(relay, struct(half, nocc + OPT["rel"], width), crossed), 1)
    chol, weight = call(
        functools.partial(place_chol, sources=sources, nocc=nocc, width=width, **sizes),
        (struct(half * LANES, wide), struct(2 * nchol, LANES, dtype=f32)),
        chol_vectors,
        paired,
        crossed,
        relayed,
        phase_codes,
    )
    term = struct(half * LANES, padded, dtype=f32)
    mine = [theta] + early
    def message(extra, span, *blocks):
        shape = (2 * nocc + extra, 2 * span)
        return call(
            functools.partial(mail, width=width), struct(*shape) if len(blocks) == 1 else struct(2, *shape), *blocks
        )

    a_ops = [swap(message(OPT["ar"], width if OPT["aw"] else padded, theta, early[0]), 1)]
    b_op = message(OPT["br"], width if OPT["bw"] else padded, early[1])
    theirs = a_ops + [swap(b_op, 1)] + [swap(t, 1) for t in early[2:]]
    grads, energies, factors = None, [], []
    for start in range(0, nchol - 1, 3):
        if start == 0 and len(a_ops) == 1:
            group, counts = mine[:3] + theirs[:2], (1, 1, 1, 2, 1)
        else:
            shift = len(a_ops) - 2
            group = mine[start:start + 3] + theirs[start + shift:start + 3 + shift]
            counts = (1,) * len(group)
        walkers = sum(counts)
        *terms, tmat, theta_s, cotan_s = call(
            functools.partial(
                first_walkers, first=start, counts=counts, walkers=walkers, nocc=nocc, width=width, **sizes
            ),
            (
                term,
                term,
                struct(walkers * LANES, half * LANES, dtype=f32),
                struct(walkers * LANES, wide),
                struct(half * LANES, walkers * LANES),
            ),
            *group,
            chol,
            weight,
        )
        energy = call(functools.partial(first_energies, half=half), struct(walkers, LANES, dtype=f32), tmat)
        grads = terms if grads is None else [a + b for a, b in zip(grads, terms)]
        energies += [(energy[:walkers // 2], energy[walkers // 2:])]
        factors += [cotan_s, theta_s]
    if len(energies) > 1:
        energy = jnp.concatenate([e[i] for i in (0, 1) for e in energies])
    theirs_last = swap(lax.optimization_barrier((last, grads[0]))[0], 1)

    walkers = 2
    same, other, energy, theta_s, cotan_s = call(
        functools.partial(last_walkers, sources=sources, nocc=nocc, width=width, **sizes),
        (
            struct(half * nocc, padded),
            struct(half * nocc, padded),
            struct(2, nchol + SPARE, LANES, dtype=f32),
            struct(walkers * LANES, wide),
            struct(half * LANES, walkers * LANES),
        ),
        last,
        theirs_last,
        chol,
        weight,
        grads[0],
        grads[1],
        energy,
    )
    same, other = swap(same, 2), swap(other, 3)
    arrived, n, flip = swap(energy, 1), nchol // 2, 1
    while n:
        energy, send = call(halve, (struct(n, LANES, dtype=f32),) * 2, energy, arrived)
        arrived = turn(send, [(i, i ^ flip) for i in range(nchol)])
        if flip == HELD:
            theta_s, _ = lax.optimization_barrier((theta_s, arrived))
        n, flip = n // 2, flip * 2
    own, *core = call(
        functools.partial(chip_walkers, nocc=nocc, **sizes),
        (struct(half, rows, padded, dtype=f32),) + (struct(half // 2 * nocc, width),) * 2,
        *factors,
        cotan_s,
        theta_s,
    )
    core = [swap(c, 1) for c in core]
    chol_grad, energies = call(
        finish,
        (struct(nocc, gdev, width, dtype=f32), struct(1, 1, dtype=f32)),
        own,
        same,
        other,
        *core,
        energy,
        arrived,
        out=HBM,
        scratch=[
            pltpu.VMEM((nocc, gdev, width), f32),
            pltpu.VMEM((1, 1), f32),
            pltpu.SemaphoreType.DMA((1 - (-nocc // STEP),)),
        ],
    )
    return jnp.swapaxes(chol_grad, 0, 1), energies


def solution(mesh):
    placed = (
        P("chol", None, "walk"),
        P(("dom", "walk"), "chol", None, None),
        P(("dom", "walk"), None),
        P(("dom", "walk"), "chol", None),
    )
    return jax.shard_map(
        functools.partial(body, nchol=mesh.shape["chol"], nwalk=mesh.shape["walk"]),
        mesh=mesh,
        in_specs=placed,
        out_specs=(P(("dom", "chol"), None, "walk"), P(("dom", "walk"), "chol")),
        check_vma=False,
    )
```

```python
import functools

import jax
import jax.numpy as jnp
from jax import lax
from jax.experimental import pallas as pl
from jax.experimental.pallas import tpu as pltpu
from jax.sharding import PartitionSpec as P

LANES = 128
STEP = 32
GRANT = 16 * 1024 * 1024
PREP = 56 * 1024 * 1024
HBM = pltpu.MemorySpace.HBM
VMEM = pltpu.MemorySpace.VMEM
bf16, f32 = jnp.bfloat16, jnp.float32


def ceil_to(value, step):
    return -(-value // step) * step


def prep_theta(occ_hbm, green_hbm, chol_hbm, out_ref, chol_ref, occ_ref, green_ref, sems, *, width, padded):
    pairs = (green_hbm, green_ref), (occ_hbm, occ_ref), (chol_hbm, chol_ref)
    copies = [pltpu.make_async_copy(source, target, sems.at[i]) for i, (source, target) in enumerate(pairs)]
    for copy in copies:
        copy.start()
    out_ref[...] = jnp.zeros_like(out_ref)
    nocc, norb = green_ref.shape
    fold = norb // width // 2
    copies[1].wait()
    row, lane = (lax.broadcasted_iota(jnp.int32, (nocc, nocc), axis) for axis in (0, 1))
    source = jnp.sum(jnp.where(row == lane, occ_ref[...], 0).astype(f32), axis=1, keepdims=True)
    pick = (source == lane.astype(f32)).astype(bf16)
    copies[0].wait()
    theta = jnp.dot(pick, green_ref[...], preferred_element_type=f32)
    for k in range(norb // width):
        row, lane = k // fold * nocc, k % fold * padded
        out_ref[row:row + nocc, lane:lane + width] = theta[:, width * k:width * (k + 1)].astype(bf16)
    copies[2].wait()


def prep_chol(chol_ref, code_ref, cross_ref):
    gdev, nocc, width = chol_ref.shape
    half = gdev // 2
    h = lax.rem(lax.axis_index("walk"), 2)
    for g in range(half):
        row, lane = g // (half // 2) * nocc, g % (half // 2) * width
        cross_ref[row:row + nocc, lane:lane + width] = chol_ref[(1 - h) * half + g]
    cross_ref[2 * nocc:, :] = jnp.zeros((1, cross_ref.shape[1]), bf16)
    cross_ref[2 * nocc:, :code_ref.shape[1]] = code_ref[...].astype(f32).astype(bf16)


def mail(*refs, width):
    *ins, out_ref = refs
    out_ref[...] = jnp.zeros_like(out_ref)
    for n, ref in enumerate(ins):
        rows, padded = ref.shape[0], ref.shape[1] // 2
        target = out_ref.at[n] if len(out_ref.shape) == 3 else out_ref
        span = target.shape[1] // 2
        for k in range(2):
            target[:rows, k * span:k * span + width] = ref[:, k * padded:k * padded + width]


def relay(crossed_ref, out_ref):
    half = crossed_ref.shape[0] // 2
    h = lax.rem(lax.axis_index("walk"), 2)
    for g in range(half):
        out_ref[g] = crossed_ref[(1 - h) * half + g]


def source_of(me, path):
    return sum(jnp.where(me == i, s, 0) for i, s in enumerate(path))


def place_chol(
    own_ref, cross_ref, same_ref, other_ref, code_ref, out_ref, weight_ref, *, sources, half, nocc, width, padded
):
    out_ref[...] = jnp.zeros_like(out_ref)
    h = lax.rem(lax.axis_index("walk"), 2)
    for g in range(half):
        row, lane = g // (half // 2) * nocc, g % (half // 2) * width
        rows = slice(g * LANES, g * LANES + nocc)
        crossed = cross_ref[row:row + nocc, lane:lane + width]
        for s, block in enumerate((own_ref[h * half + g], crossed, same_ref[h * half + g], other_ref[g])):
            out_ref[rows, column(s, padded)] = jnp.pad(block, ((0, 0), (0, padded - width)))
    nchol = code_ref.shape[1]
    me = lax.axis_index("chol")
    mine = code_ref[...].astype(f32)
    theirs = cross_ref[2 * nocc:, :nchol].astype(f32)
    codes = jnp.zeros(weight_ref.shape, f32)
    at = lax.broadcasted_iota(jnp.int32, codes.shape, 0)
    for n, path in enumerate(sources):
        source = source_of(me, path)
        for group, values in enumerate((mine, theirs)):
            here = lax.broadcasted_iota(jnp.int32, values.shape, 1) == source
            code = jnp.sum(jnp.where(here, values, 0.0), axis=1, keepdims=True)
            codes = jnp.where(at == group * nchol + n, code, codes)
    weight_ref[...] = -jnp.cos(jnp.pi * codes / 4.0)


def column(s, padded):
    return pl.ds(pl.multiple_of((lax.axis_index("walk") ^ s) * padded, padded), padded)


def place_theta(thetas, theta_s, nocc, width, padded):
    theta_s[...] = jnp.zeros_like(theta_s)
    for w, (ref, n) in enumerate(thetas):
        theta = ref[n] if len(ref.shape) == 3 else ref[...]
        span = theta.shape[1] // 2
        rows = slice(w * LANES, w * LANES + nocc)
        for i in range(2):
            part = theta[i * nocc:(i + 1) * nocc]
            if span == padded:
                theta_s[rows, 2 * i * padded:2 * (i + 1) * padded] = part
            else:
                for k in range(2):
                    lane = (2 * i + k) * padded
                    theta_s[rows, lane:lane + width] = part[:, k * span:k * span + width]


def first_walkers(*refs, first, counts, walkers, half, nocc, width, padded):
    counts = list(counts)
    *thetas, chol_s, weight_ref, same_ref, other_ref, tmat_ref, theta_s, cotan_s = refs
    place_theta([(ref, n) for ref in thetas for n in range(counts.pop(0))], theta_s, nocc, width, padded)
    tmat = lax.dot_general(theta_s[...], chol_s[...], (((1,), (1,)), ((), ())), preferred_element_type=f32)
    tmat_ref[...] = tmat
    n = walkers // 2
    for w in range(walkers):
        row = w // n * (weight_ref.shape[0] // 2) + first + w % n
        weight = weight_ref[row:row + 1, :]
        for g in range(half):
            block = tmat[w * LANES:(w + 1) * LANES, g * LANES:(g + 1) * LANES]
            cotan_s[g * LANES:(g + 1) * LANES, w * LANES:(w + 1) * LANES] = (weight * block).astype(bf16)
    for s, ref in ((2, same_ref), (3, other_ref)):
        ref[...] = jnp.dot(cotan_s[...], theta_s[:, column(s, padded)], preferred_element_type=f32)


def first_energies(tmat_ref, energy_ref, *, half):
    for w in range(energy_ref.shape[0]):
        total = jnp.zeros((LANES, LANES), f32)
        for g in range(half):
            block = tmat_ref[w * LANES:(w + 1) * LANES, g * LANES:(g + 1) * LANES]
            total += block * block.T
        energy_ref[w:w + 1, :] = -0.5 * jnp.sum(total, axis=0, keepdims=True)


def last_walkers(
    mine, theirs, chol_s, weight_ref, same_part, other_part, first_ref, same_ref, other_ref, energy_ref, theta_s, cotan_s,
    *, sources, half, nocc, width, padded
):
    place_theta([(mine, 0), (theirs, 0)], theta_s, nocc, width, padded)
    tmat = lax.dot_general(theta_s[...], chol_s[...], (((1,), (1,)), ((), ())), preferred_element_type=f32)
    for w in range(2):
        row = (w + 1) * (weight_ref.shape[0] // 2) - 1
        weight = weight_ref[row:row + 1, :]
        for g in range(half):
            block = tmat[w * LANES:(w + 1) * LANES, g * LANES:(g + 1) * LANES]
            cotan_s[g * LANES:(g + 1) * LANES, w * LANES:(w + 1) * LANES] = (weight * block).astype(bf16)
    for ref, part, s in ((same_ref, same_part, 2), (other_ref, other_part, 3)):
        grad = part[...] + jnp.dot(cotan_s[...], theta_s[:, column(s, padded)], preferred_element_type=f32)
        store_grad(grad, ref, half, nocc)
    early = first_ref.shape[0] // 2
    me = lax.axis_index("chol")
    rows = [pl.ds(me ^ source_of(me, path), 1) for path in sources]
    for w in range(2):
        total = jnp.zeros((LANES, LANES), f32)
        for g in range(half):
            block = tmat[w * LANES:(w + 1) * LANES, g * LANES:(g + 1) * LANES]
            total += block * block.T
        for n in range(early):
            energy_ref[w, rows[n], :] = first_ref[w * early + n:w * early + n + 1]
        energy_ref[w, rows[early], :] = -0.5 * jnp.sum(total, axis=0, keepdims=True)


def store_grad(grad, ref, half, nocc):
    for g in range(half):
        if len(ref.shape) == 2:
            ref[g * nocc:(g + 1) * nocc] = grad[g * LANES:g * LANES + nocc, :ref.shape[1]].astype(ref.dtype)
        else:
            ref[g] = grad[g * LANES:g * LANES + ref.shape[1]].astype(ref.dtype)


def chip_walkers(*refs, half, nocc, padded):
    *factors, own_ref, core_ref = refs
    for s in (1, 0):
        grad = 0.0
        for cotan_s, theta_s in zip(factors[::2], factors[1::2]):
            grad += jnp.dot(cotan_s[...], theta_s[:, column(s, padded)], preferred_element_type=f32)
        store_grad(grad, core_ref if s else own_ref, half, nocc)


def halve(mine_ref, arrived_ref, keep_ref, send_ref):
    ours, theirs = (ref.at[i] if len(ref.shape) == 3 else ref for i, ref in enumerate((mine_ref, arrived_ref)))
    for n in range(keep_ref.shape[0]):
        for ref, row in ((keep_ref, 2 * n), (send_ref, 2 * n + 1)):
            ref[n:n + 1, :] = ours[row:row + 1, :] + theirs[row:row + 1, :]


def finish(*refs):
    *refs, out_hbm, energy_hbm, out_ref, energy_ref, sems = refs
    own_ref, same_ref, other_ref, core_ref, *energy_refs = refs
    half = own_ref.shape[0]
    nocc, gdev, width = out_ref.shape
    h = lax.rem(lax.axis_index("walk"), 2)
    energy = sum(ref[...] for ref in energy_refs)
    energy_ref[...] = jnp.sum(energy, axis=1, keepdims=True)
    copies = [pltpu.make_async_copy(energy_ref, energy_hbm, sems.at[0])]
    copies[0].start()

    def arrived(*refs):
        n = half // len(refs)
        blocks = [ref[g * nocc + start:g * nocc + stop, :width] for ref in refs for g in range(n)]
        return jnp.stack([block.astype(f32) for block in blocks])

    for n, start in enumerate(range(0, nocc, STEP), start=1):
        stop = min(start + STEP, nocc)
        mine = own_ref[:, start:stop, :width] + arrived(same_ref)
        theirs = arrived(core_ref) + arrived(other_ref)

        @pl.when(h == 0)
        def _():
            out_ref[start:stop] = jnp.swapaxes(jnp.concatenate([mine, theirs], axis=0), 0, 1)

        @pl.when(h == 1)
        def _():
            out_ref[start:stop] = jnp.swapaxes(jnp.concatenate([theirs, mine], axis=0), 0, 1)

        copies.append(pltpu.make_async_copy(out_ref.at[start:stop], out_hbm.at[start:stop], sems.at[n]))
        copies[-1].start()
    for copy in copies:
        copy.wait()


def call(kernel, outs, *operands, scratch=(), ins=VMEM, out=VMEM, grant=GRANT):
    return pl.pallas_call(
        kernel,
        out_shape=outs,
        in_specs=[pl.BlockSpec(memory_space=ins)] * len(operands),
        out_specs=jax.tree.map(lambda _: pl.BlockSpec(memory_space=out), outs),
        scratch_shapes=scratch,
        compiler_params=pltpu.CompilerParams(vmem_limit_bytes=grant),
    )(*operands)


def body(chol_vectors, green_blocks, phase_codes, occupations, *, nchol, nwalk):
    gdev, nocc, width = chol_vectors.shape
    norb = green_blocks.shape[3]
    half = gdev // 2
    rows = ceil_to(nocc, 8)
    padded = ceil_to(width, LANES)
    wide = padded * nwalk
    sizes = dict(half=half, padded=padded)

    def swap(x, flip):
        return lax.ppermute(x, "walk", [(i, i ^ flip) for i in range(nwalk)])

    def turn(x, pairs):
        return lax.ppermute(x, "chol", pairs)

    def struct(*shape, dtype=bf16):
        return jax.ShapeDtypeStruct(shape, dtype)

    block = struct(2 * nocc, wide // 2)
    theta, chol_vectors = call(
        functools.partial(prep_theta, width=width, padded=padded),
        (pltpu.VMEM(block.shape, bf16), pltpu.VMEM((nocc, gdev, width), bf16)),
        occupations.reshape(1, nocc),
        green_blocks.reshape(nocc, norb),
        jnp.swapaxes(chol_vectors, 0, 1),
        scratch=[pltpu.VMEM((1, nocc), jnp.int32), pltpu.VMEM((nocc, norb), bf16), pltpu.SemaphoreType.DMA((3,))],
        ins=HBM,
        grant=PREP,
    )
    chol_vectors = jnp.swapaxes(chol_vectors, 0, 1)
    cross = call(prep_chol, struct(2 * nocc + 1, half // 2 * width), chol_vectors, phase_codes)

    if nchol == 4:
        there = [(0, 2), (2, 3), (3, 1), (1, 0)]
        back = [(b, a) for a, b in there]
        paths = [there, back, [(i, 3 - i) for i in range(4)]]
        first = turn(theta, there)
        early = [first, turn(theta, back)]
        last = turn(first, there)
    else:
        paths = [[(i, (i + d) % nchol) for i in range(nchol)] for d in range(1, nchol)]
        *early, last = [turn(theta, path) for path in paths]
    sources = [list(range(nchol))] + [[a for a, _ in sorted(path, key=lambda p: p[1])] for path in paths]

    paired = swap(cross, 1)
    crossed = swap(chol_vectors, 2)
    relayed = swap(call(relay, struct(half, nocc, width), crossed), 1)
    chol, weight = call(
        functools.partial(place_chol, sources=sources, nocc=nocc, width=width, **sizes),
        (struct(half * LANES, wide), struct(2 * nchol, LANES, dtype=f32)),
        chol_vectors,
        paired,
        crossed,
        relayed,
        phase_codes,
    )
    term = struct(half * LANES, padded, dtype=f32)
    mine = [theta] + early
    def message(extra, span, *blocks):
        shape = (2 * nocc + extra, 2 * span)
        return call(
            functools.partial(mail, width=width), struct(*shape) if len(blocks) == 1 else struct(2, *shape), *blocks
        )

    a_ops = [swap(message(2, width, theta, early[0]), 1)]
    b_op = message(4, width, early[1])
    theirs = a_ops + [swap(b_op, 1)] + [swap(t, 1) for t in early[2:]]
    grads, energies, factors = None, [], []
    for start in range(0, nchol - 1, 3):
        if start == 0 and len(a_ops) == 1:
            group, counts = mine[:3] + theirs[:2], (1, 1, 1, 2, 1)
        else:
            shift = len(a_ops) - 2
            group = mine[start:start + 3] + theirs[start + shift:start + 3 + shift]
            counts = (1,) * len(group)
        walkers = sum(counts)
        *terms, tmat, theta_s, cotan_s = call(
            functools.partial(
                first_walkers, first=start, counts=counts, walkers=walkers, nocc=nocc, width=width, **sizes
            ),
            (
                term,
                term,
                struct(walkers * LANES, half * LANES, dtype=f32),
                struct(walkers * LANES, wide),
                struct(half * LANES, walkers * LANES),
            ),
            *group,
            chol,
            weight,
        )
        energy = call(functools.partial(first_energies, half=half), struct(walkers, LANES, dtype=f32), tmat)
        grads = terms if grads is None else [a + b for a, b in zip(grads, terms)]
        energies += [(energy[:walkers // 2], energy[walkers // 2:])]
        factors += [cotan_s, theta_s]
    if len(energies) > 1:
        energy = jnp.concatenate([e[i] for i in (0, 1) for e in energies])
    theirs_last = swap(lax.optimization_barrier((last, grads[0]))[0], 1)

    walkers = 2
    same, other, energy, theta_s, cotan_s = call(
        functools.partial(last_walkers, sources=sources, nocc=nocc, width=width, **sizes),
        (
            struct(half * nocc, padded),
            struct(half * nocc, width),
            struct(2, nchol, LANES, dtype=f32),
            struct(walkers * LANES, wide),
            struct(half * LANES, walkers * LANES),
        ),
        last,
        theirs_last,
        chol,
        weight,
        grads[0],
        grads[1],
        energy,
    )
    same, other = swap(same, 2), swap(other, 3)
    arrived, n, flip = swap(energy, 1), nchol // 2, 1
    while n:
        energy, send = call(halve, (struct(n, LANES, dtype=f32),) * 2, energy, arrived)
        arrived = turn(send, [(i, i ^ flip) for i in range(nchol)])
        if flip == 1:
            first_in = arrived
        n, flip = n // 2, flip * 2
    own, *core = call(
        functools.partial(chip_walkers, nocc=nocc, **sizes),
        (struct(half, rows, padded, dtype=f32), struct(half * nocc, width)),
        *factors,
        cotan_s,
        theta_s,
    )
    core = [swap(c, 1) for c in lax.optimization_barrier((*core, first_in))[:-1]]
    chol_grad, energies = call(
        finish,
        (struct(nocc, gdev, width, dtype=f32), struct(1, 1, dtype=f32)),
        own,
        same,
        other,
        *core,
        energy,
        arrived,
        out=HBM,
        scratch=[
            pltpu.VMEM((nocc, gdev, width), f32),
            pltpu.VMEM((1, 1), f32),
            pltpu.SemaphoreType.DMA((1 - (-nocc // STEP),)),
        ],
    )
    return jnp.swapaxes(chol_grad, 0, 1), energies


def solution(mesh):
    placed = (
        P("chol", None, "walk"),
        P(("dom", "walk"), "chol", None, None),
        P(("dom", "walk"), None),
        P(("dom", "walk"), "chol", None),
    )
    return jax.shard_map(
        functools.partial(body, nchol=mesh.shape["chol"], nwalk=mesh.shape["walk"]),
        mesh=mesh,
        in_specs=placed,
        out_specs=(P(("dom", "chol"), None, "walk"), P(("dom", "walk"), "chol")),
        check_vma=False,
    )
```

```python
import functools

import jax
import jax.numpy as jnp
from jax import lax
from jax.experimental import pallas as pl
from jax.experimental.pallas import tpu as pltpu
from jax.sharding import PartitionSpec as P

LANES = 128
STEP = 32
SPARE = 104
OPT = {'aw': 1, 'bw': 1, 'ar': 2, 'br': 4, 'rel': 0, 'hold': 1, 'c1r': 0}
GRANT = 16 * 1024 * 1024
PREP = 56 * 1024 * 1024
HBM = pltpu.MemorySpace.HBM
VMEM = pltpu.MemorySpace.VMEM
bf16, f32 = jnp.bfloat16, jnp.float32


def ceil_to(value, step):
    return -(-value // step) * step


def prep_theta(occ_hbm, green_hbm, chol_hbm, out_ref, chol_ref, occ_ref, green_ref, sems, *, width, padded):
    pairs = (green_hbm, green_ref), (occ_hbm, occ_ref), (chol_hbm, chol_ref)
    copies = [pltpu.make_async_copy(source, target, sems.at[i]) for i, (source, target) in enumerate(pairs)]
    for copy in copies:
        copy.start()
    out_ref[...] = jnp.zeros_like(out_ref)
    nocc, norb = green_ref.shape
    fold = norb // width // 2
    copies[1].wait()
    row, lane = (lax.broadcasted_iota(jnp.int32, (nocc, nocc), axis) for axis in (0, 1))
    source = jnp.sum(jnp.where(row == lane, occ_ref[...], 0).astype(f32), axis=1, keepdims=True)
    pick = (source == lane.astype(f32)).astype(bf16)
    copies[0].wait()
    theta = jnp.dot(pick, green_ref[...], preferred_element_type=f32)
    for k in range(norb // width):
        row, lane = k // fold * nocc, k % fold * padded
        out_ref[row:row + nocc, lane:lane + width] = theta[:, width * k:width * (k + 1)].astype(bf16)
    copies[2].wait()


def prep_chol(chol_ref, code_ref, cross_ref):
    gdev, nocc, width = chol_ref.shape
    half = gdev // 2
    h = lax.rem(lax.axis_index("walk"), 2)
    for g in range(half):
        row, lane = g // (half // 2) * nocc, g % (half // 2) * width
        cross_ref[row:row + nocc, lane:lane + width] = chol_ref[(1 - h) * half + g]
    cross_ref[2 * nocc:, :] = jnp.zeros((1, cross_ref.shape[1]), bf16)
    cross_ref[2 * nocc:, :code_ref.shape[1]] = code_ref[...].astype(f32).astype(bf16)


def mail(*refs, width):
    *ins, out_ref = refs
    out_ref[...] = jnp.zeros_like(out_ref)
    for n, ref in enumerate(ins):
        rows, padded = ref.shape[0], ref.shape[1] // 2
        target = out_ref.at[n] if len(out_ref.shape) == 3 else out_ref
        span = target.shape[1] // 2
        for k in range(2):
            target[:rows, k * span:k * span + width] = ref[:, k * padded:k * padded + width]


def relay(crossed_ref, out_ref):
    half = crossed_ref.shape[0] // 2
    h = lax.rem(lax.axis_index("walk"), 2)
    for g in range(half):
        out_ref[g] = crossed_ref[(1 - h) * half + g]


def source_of(me, path):
    return sum(jnp.where(me == i, s, 0) for i, s in enumerate(path))


def place_chol(
    own_ref, cross_ref, same_ref, other_ref, code_ref, out_ref, weight_ref, *, sources, half, nocc, width, padded
):
    out_ref[...] = jnp.zeros_like(out_ref)
    h = lax.rem(lax.axis_index("walk"), 2)
    for g in range(half):
        row, lane = g // (half // 2) * nocc, g % (half // 2) * width
        rows = slice(g * LANES, g * LANES + nocc)
        crossed = cross_ref[row:row + nocc, lane:lane + width]
        for s, block in enumerate((own_ref[h * half + g], crossed, same_ref[h * half + g], other_ref[g])):
            out_ref[rows, column(s, padded)] = jnp.pad(block, ((0, 0), (0, padded - width)))
    nchol = code_ref.shape[1]
    me = lax.axis_index("chol")
    mine = code_ref[...].astype(f32)
    theirs = cross_ref[2 * nocc:, :nchol].astype(f32)
    codes = jnp.zeros(weight_ref.shape, f32)
    at = lax.broadcasted_iota(jnp.int32, codes.shape, 0)
    for n, path in enumerate(sources):
        source = source_of(me, path)
        for group, values in enumerate((mine, theirs)):
            here = lax.broadcasted_iota(jnp.int32, values.shape, 1) == source
            code = jnp.sum(jnp.where(here, values, 0.0), axis=1, keepdims=True)
            codes = jnp.where(at == group * nchol + n, code, codes)
    weight_ref[...] = -jnp.cos(jnp.pi * codes / 4.0)


def column(s, padded):
    return pl.ds(pl.multiple_of((lax.axis_index("walk") ^ s) * padded, padded), padded)


def place_theta(thetas, theta_s, nocc, width, padded):
    theta_s[...] = jnp.zeros_like(theta_s)
    for w, (ref, n) in enumerate(thetas):
        theta = ref[n] if len(ref.shape) == 3 else ref[...]
        span = theta.shape[1] // 2
        rows = slice(w * LANES, w * LANES + nocc)
        for i in range(2):
            part = theta[i * nocc:(i + 1) * nocc]
            if span == padded:
                theta_s[rows, 2 * i * padded:2 * (i + 1) * padded] = part
            else:
                for k in range(2):
                    lane = (2 * i + k) * padded
                    theta_s[rows, lane:lane + width] = part[:, k * span:k * span + width]


def first_walkers(*refs, first, counts, walkers, half, nocc, width, padded):
    counts = list(counts)
    *thetas, chol_s, weight_ref, same_ref, other_ref, tmat_ref, theta_s, cotan_s = refs
    place_theta([(ref, n) for ref in thetas for n in range(counts.pop(0))], theta_s, nocc, width, padded)
    tmat = lax.dot_general(theta_s[...], chol_s[...], (((1,), (1,)), ((), ())), preferred_element_type=f32)
    tmat_ref[...] = tmat
    n = walkers // 2
    for w in range(walkers):
        row = w // n * (weight_ref.shape[0] // 2) + first + w % n
        weight = weight_ref[row:row + 1, :]
        for g in range(half):
            block = tmat[w * LANES:(w + 1) * LANES, g * LANES:(g + 1) * LANES]
            cotan_s[g * LANES:(g + 1) * LANES, w * LANES:(w + 1) * LANES] = (weight * block).astype(bf16)
    for s, ref in ((2, same_ref), (3, other_ref)):
        ref[...] = jnp.dot(cotan_s[...], theta_s[:, column(s, padded)], preferred_element_type=f32)


def first_energies(tmat_ref, energy_ref, *, half):
    for w in range(energy_ref.shape[0]):
        total = jnp.zeros((LANES, LANES), f32)
        for g in range(half):
            block = tmat_ref[w * LANES:(w + 1) * LANES, g * LANES:(g + 1) * LANES]
            total += block * block.T
        energy_ref[w:w + 1, :] = -0.5 * jnp.sum(total, axis=0, keepdims=True)


def last_walkers(
    mine, theirs, chol_s, weight_ref, same_part, other_part, first_ref, same_ref, other_ref, energy_ref, theta_s, cotan_s,
    *, sources, half, nocc, width, padded
):
    place_theta([(mine, 0), (theirs, 0)], theta_s, nocc, width, padded)
    tmat = lax.dot_general(theta_s[...], chol_s[...], (((1,), (1,)), ((), ())), preferred_element_type=f32)
    for w in range(2):
        row = (w + 1) * (weight_ref.shape[0] // 2) - 1
        weight = weight_ref[row:row + 1, :]
        for g in range(half):
            block = tmat[w * LANES:(w + 1) * LANES, g * LANES:(g + 1) * LANES]
            cotan_s[g * LANES:(g + 1) * LANES, w * LANES:(w + 1) * LANES] = (weight * block).astype(bf16)
    for ref, part, s in ((same_ref, same_part, 2), (other_ref, other_part, 3)):
        grad = part[...] + jnp.dot(cotan_s[...], theta_s[:, column(s, padded)], preferred_element_type=f32)
        store_grad(grad, ref, half, nocc)
    energy_ref[...] = jnp.zeros_like(energy_ref)
    early = first_ref.shape[0] // 2
    me = lax.axis_index("chol")
    rows = [pl.ds(me ^ source_of(me, path), 1) for path in sources]
    for w in range(2):
        total = jnp.zeros((LANES, LANES), f32)
        for g in range(half):
            block = tmat[w * LANES:(w + 1) * LANES, g * LANES:(g + 1) * LANES]
            total += block * block.T
        for n in range(early):
            energy_ref[w, rows[n], :] = first_ref[w * early + n:w * early + n + 1]
        energy_ref[w, rows[early], :] = -0.5 * jnp.sum(total, axis=0, keepdims=True)


def store_grad(grad, ref, half, nocc):
    for g in range(half):
        if len(ref.shape) == 2:
            ref[g * nocc:(g + 1) * nocc] = grad[g * LANES:g * LANES + nocc, :ref.shape[1]].astype(ref.dtype)
        else:
            ref[g] = grad[g * LANES:g * LANES + ref.shape[1]].astype(ref.dtype)


def chip_walkers(*refs, half, nocc, padded):
    *factors, own_ref, low_ref, high_ref = refs
    for s in (1, 0):
        grad = 0.0
        for cotan_s, theta_s in zip(factors[::2], factors[1::2]):
            grad += jnp.dot(cotan_s[...], theta_s[:, column(s, padded)], preferred_element_type=f32)
        if s == 0:
            store_grad(grad, own_ref, half, nocc)
        else:
            store_grad(grad, low_ref, half // 2, nocc)
            store_grad(grad[half // 2 * LANES:], high_ref, half // 2, nocc)


def halve(mine_ref, arrived_ref, keep_ref, send_ref):
    ours, theirs = (ref.at[i] if len(ref.shape) == 3 else ref for i, ref in enumerate((mine_ref, arrived_ref)))
    for n in range(keep_ref.shape[0]):
        for ref, row in ((keep_ref, 2 * n), (send_ref, 2 * n + 1)):
            ref[n:n + 1, :] = ours[row:row + 1, :] + theirs[row:row + 1, :]


def finish(*refs):
    *refs, out_hbm, energy_hbm, out_ref, energy_ref, sems = refs
    own_ref, same_ref, other_ref, low_ref, high_ref, *energy_refs = refs
    half = own_ref.shape[0]
    nocc, gdev, width = out_ref.shape
    h = lax.rem(lax.axis_index("walk"), 2)
    energy = sum(ref[...] for ref in energy_refs)
    energy_ref[...] = jnp.sum(energy, axis=1, keepdims=True)
    copies = [pltpu.make_async_copy(energy_ref, energy_hbm, sems.at[0])]
    copies[0].start()

    def arrived(*refs):
        n = half // len(refs)
        blocks = [ref[g * nocc + start:g * nocc + stop, :width] for ref in refs for g in range(n)]
        return jnp.stack([block.astype(f32) for block in blocks])

    for n, start in enumerate(range(0, nocc, STEP), start=1):
        stop = min(start + STEP, nocc)
        mine = own_ref[:, start:stop, :width] + arrived(same_ref)
        theirs = arrived(low_ref, high_ref) + arrived(other_ref)

        @pl.when(h == 0)
        def _():
            out_ref[start:stop] = jnp.swapaxes(jnp.concatenate([mine, theirs], axis=0), 0, 1)

        @pl.when(h == 1)
        def _():
            out_ref[start:stop] = jnp.swapaxes(jnp.concatenate([theirs, mine], axis=0), 0, 1)

        copies.append(pltpu.make_async_copy(out_ref.at[start:stop], out_hbm.at[start:stop], sems.at[n]))
        copies[-1].start()
    for copy in copies:
        copy.wait()


def call(kernel, outs, *operands, scratch=(), ins=VMEM, out=VMEM, grant=GRANT):
    return pl.pallas_call(
        kernel,
        out_shape=outs,
        in_specs=[pl.BlockSpec(memory_space=ins)] * len(operands),
        out_specs=jax.tree.map(lambda _: pl.BlockSpec(memory_space=out), outs),
        scratch_shapes=scratch,
        compiler_params=pltpu.CompilerParams(vmem_limit_bytes=grant),
    )(*operands)


def body(chol_vectors, green_blocks, phase_codes, occupations, *, nchol, nwalk):
    gdev, nocc, width = chol_vectors.shape
    norb = green_blocks.shape[3]
    half = gdev // 2
    rows = ceil_to(nocc, 8)
    padded = ceil_to(width, LANES)
    wide = padded * nwalk
    sizes = dict(half=half, padded=padded)

    def swap(x, flip):
        return lax.ppermute(x, "walk", [(i, i ^ flip) for i in range(nwalk)])

    def turn(x, pairs):
        return lax.ppermute(x, "chol", pairs)

    def struct(*shape, dtype=bf16):
        return jax.ShapeDtypeStruct(shape, dtype)

    block = struct(2 * nocc, wide // 2)
    theta, chol_vectors = call(
        functools.partial(prep_theta, width=width, padded=padded),
        (pltpu.VMEM(block.shape, bf16), pltpu.VMEM((nocc, gdev, width), bf16)),
        occupations.reshape(1, nocc),
        green_blocks.reshape(nocc, norb),
        jnp.swapaxes(chol_vectors, 0, 1),
        scratch=[pltpu.VMEM((1, nocc), jnp.int32), pltpu.VMEM((nocc, norb), bf16), pltpu.SemaphoreType.DMA((3,))],
        ins=HBM,
        grant=PREP,
    )
    chol_vectors = jnp.swapaxes(chol_vectors, 0, 1)
    cross = call(prep_chol, struct(2 * nocc + 1, half // 2 * width), chol_vectors, phase_codes)

    if nchol == 4:
        there = [(0, 2), (2, 3), (3, 1), (1, 0)]
        back = [(b, a) for a, b in there]
        paths = [there, back, [(i, 3 - i) for i in range(4)]]
        first = turn(theta, there)
        early = [first, turn(theta, back)]
        last = turn(first, there)
    else:
        paths = [[(i, (i + d) % nchol) for i in range(nchol)] for d in range(1, nchol)]
        *early, last = [turn(theta, path) for path in paths]
    sources = [list(range(nchol))] + [[a for a, _ in sorted(path, key=lambda p: p[1])] for path in paths]

    paired = swap(cross, 1)
    crossed = swap(chol_vectors, 2)
    relayed = swap(call(relay, struct(half, nocc + OPT["rel"], width), crossed), 1)
    chol, weight = call(
        functools.partial(place_chol, sources=sources, nocc=nocc, width=width, **sizes),
        (struct(half * LANES, wide), struct(2 * nchol, LANES, dtype=f32)),
        chol_vectors,
        paired,
        crossed,
        relayed,
        phase_codes,
    )
    term = struct(half * LANES, padded, dtype=f32)
    mine = [theta] + early
    def message(extra, span, *blocks):
        shape = (2 * nocc + extra, 2 * span)
        return call(
            functools.partial(mail, width=width), struct(*shape) if len(blocks) == 1 else struct(2, *shape), *blocks
        )

    a_ops = [swap(message(OPT["ar"], width if OPT["aw"] else padded, theta, early[0]), 1)]
    b_op = message(OPT["br"], width if OPT["bw"] else padded, early[1])
    theirs = a_ops + [swap(b_op, 1)] + [swap(t, 1) for t in early[2:]]
    grads, energies, factors = None, [], []
    for start in range(0, nchol - 1, 3):
        if start == 0 and len(a_ops) == 1:
            group, counts = mine[:3] + theirs[:2], (1, 1, 1, 2, 1)
        else:
            shift = len(a_ops) - 2
            group = mine[start:start + 3] + theirs[start + shift:start + 3 + shift]
            counts = (1,) * len(group)
        walkers = sum(counts)
        *terms, tmat, theta_s, cotan_s = call(
            functools.partial(
                first_walkers, first=start, counts=counts, walkers=walkers, nocc=nocc, width=width, **sizes
            ),
            (
                term,
                term,
                struct(walkers * LANES, half * LANES, dtype=f32),
                struct(walkers * LANES, wide),
                struct(half * LANES, walkers * LANES),
            ),
            *group,
            chol,
            weight,
        )
        energy = call(functools.partial(first_energies, half=half), struct(walkers, LANES, dtype=f32), tmat)
        grads = terms if grads is None else [a + b for a, b in zip(grads, terms)]
        energies += [(energy[:walkers // 2], energy[walkers // 2:])]
        factors += [cotan_s, theta_s]
    if len(energies) > 1:
        energy = jnp.concatenate([e[i] for i in (0, 1) for e in energies])
    theirs_last = swap(lax.optimization_barrier((last, grads[0]))[0], 1)

    walkers = 2
    same, other, energy, theta_s, cotan_s = call(
        functools.partial(last_walkers, sources=sources, nocc=nocc, width=width, **sizes),
        (
            struct(half * nocc, padded),
            struct(half * nocc, width),
            struct(2, nchol + SPARE, LANES, dtype=f32),
            struct(walkers * LANES, wide),
            struct(half * LANES, walkers * LANES),
        ),
        last,
        theirs_last,
        chol,
        weight,
        grads[0],
        grads[1],
        energy,
    )
    same, other = swap(same, 2), swap(other, 3)
    arrived, n, flip = swap(energy, 1), nchol // 2, 1
    while n:
        energy, send = call(halve, (struct(n, LANES, dtype=f32),) * 2, energy, arrived)
        arrived = turn(send, [(i, i ^ flip) for i in range(nchol)])
        if flip == 1:
            first_in = arrived
        n, flip = n // 2, flip * 2
    own, *core = call(
        functools.partial(chip_walkers, nocc=nocc, **sizes),
        (struct(half, rows, padded, dtype=f32),) + (struct(half // 2 * nocc, width),) * 2,
        *factors,
        cotan_s,
        theta_s,
    )
    core = [swap(c, 1) for c in lax.optimization_barrier((*core, first_in))[:-1]]
    chol_grad, energies = call(
        finish,
        (struct(nocc, gdev, width, dtype=f32), struct(1, 1, dtype=f32)),
        own,
        same,
        other,
        *core,
        energy,
        arrived,
        out=HBM,
        scratch=[
            pltpu.VMEM((nocc, gdev, width), f32),
            pltpu.VMEM((1, 1), f32),
            pltpu.SemaphoreType.DMA((1 - (-nocc // STEP),)),
        ],
    )
    return jnp.swapaxes(chol_grad, 0, 1), energies


def solution(mesh):
    placed = (
        P("chol", None, "walk"),
        P(("dom", "walk"), "chol", None, None),
        P(("dom", "walk"), None),
        P(("dom", "walk"), "chol", None),
    )
    return jax.shard_map(
        functools.partial(body, nchol=mesh.shape["chol"], nwalk=mesh.shape["walk"]),
        mesh=mesh,
        in_specs=placed,
        out_specs=(P(("dom", "chol"), None, "walk"), P(("dom", "walk"), "chol")),
        check_vma=False,
    )
```

```python
import functools

import jax
import jax.numpy as jnp
from jax import lax
from jax.experimental import pallas as pl
from jax.experimental.pallas import tpu as pltpu
from jax.sharding import PartitionSpec as P

LANES = 128
STEP = 32
SPARE = 104
OPT = {'aw': 1, 'bw': 1, 'ar': 2, 'br': 4, 'rel': 0, 'hold': 1, 'c1r': 0}
GRANT = 16 * 1024 * 1024
PREP = 56 * 1024 * 1024
HBM = pltpu.MemorySpace.HBM
VMEM = pltpu.MemorySpace.VMEM
bf16, f32 = jnp.bfloat16, jnp.float32


def ceil_to(value, step):
    return -(-value // step) * step


def prep_theta(occ_hbm, green_hbm, chol_hbm, out_ref, chol_ref, occ_ref, green_ref, sems, *, width, padded):
    pairs = (green_hbm, green_ref), (occ_hbm, occ_ref), (chol_hbm, chol_ref)
    copies = [pltpu.make_async_copy(source, target, sems.at[i]) for i, (source, target) in enumerate(pairs)]
    for copy in copies:
        copy.start()
    out_ref[...] = jnp.zeros_like(out_ref)
    nocc, norb = green_ref.shape
    fold = norb // width // 2
    copies[1].wait()
    row, lane = (lax.broadcasted_iota(jnp.int32, (nocc, nocc), axis) for axis in (0, 1))
    source = jnp.sum(jnp.where(row == lane, occ_ref[...], 0).astype(f32), axis=1, keepdims=True)
    pick = (source == lane.astype(f32)).astype(bf16)
    copies[0].wait()
    theta = jnp.dot(pick, green_ref[...], preferred_element_type=f32)
    for k in range(norb // width):
        row, lane = k // fold * nocc, k % fold * padded
        out_ref[row:row + nocc, lane:lane + width] = theta[:, width * k:width * (k + 1)].astype(bf16)
    copies[2].wait()


def prep_chol(chol_ref, code_ref, cross_ref):
    gdev, nocc, width = chol_ref.shape
    half = gdev // 2
    h = lax.rem(lax.axis_index("walk"), 2)
    for g in range(half):
        row, lane = g // (half // 2) * nocc, g % (half // 2) * width
        cross_ref[row:row + nocc, lane:lane + width] = chol_ref[(1 - h) * half + g]
    cross_ref[2 * nocc:, :] = jnp.zeros((1, cross_ref.shape[1]), bf16)
    cross_ref[2 * nocc:, :code_ref.shape[1]] = code_ref[...].astype(f32).astype(bf16)


def mail(*refs, width):
    *ins, out_ref = refs
    out_ref[...] = jnp.zeros_like(out_ref)
    for n, ref in enumerate(ins):
        rows, padded = ref.shape[0], ref.shape[1] // 2
        target = out_ref.at[n] if len(out_ref.shape) == 3 else out_ref
        span = target.shape[1] // 2
        for k in range(2):
            target[:rows, k * span:k * span + width] = ref[:, k * padded:k * padded + width]


def relay(crossed_ref, out_ref):
    half = crossed_ref.shape[0] // 2
    h = lax.rem(lax.axis_index("walk"), 2)
    for g in range(half):
        out_ref[g] = crossed_ref[(1 - h) * half + g]


def source_of(me, path):
    return sum(jnp.where(me == i, s, 0) for i, s in enumerate(path))


def place_chol(
    own_ref, cross_ref, same_ref, other_ref, code_ref, out_ref, weight_ref, *, sources, half, nocc, width, padded
):
    out_ref[...] = jnp.zeros_like(out_ref)
    h = lax.rem(lax.axis_index("walk"), 2)
    for g in range(half):
        row, lane = g // (half // 2) * nocc, g % (half // 2) * width
        rows = slice(g * LANES, g * LANES + nocc)
        crossed = cross_ref[row:row + nocc, lane:lane + width]
        for s, block in enumerate((own_ref[h * half + g], crossed, same_ref[h * half + g], other_ref[g])):
            out_ref[rows, column(s, padded)] = jnp.pad(block, ((0, 0), (0, padded - width)))
    nchol = code_ref.shape[1]
    me = lax.axis_index("chol")
    mine = code_ref[...].astype(f32)
    theirs = cross_ref[2 * nocc:, :nchol].astype(f32)
    codes = jnp.zeros(weight_ref.shape, f32)
    at = lax.broadcasted_iota(jnp.int32, codes.shape, 0)
    for n, path in enumerate(sources):
        source = source_of(me, path)
        for group, values in enumerate((mine, theirs)):
            here = lax.broadcasted_iota(jnp.int32, values.shape, 1) == source
            code = jnp.sum(jnp.where(here, values, 0.0), axis=1, keepdims=True)
            codes = jnp.where(at == group * nchol + n, code, codes)
    weight_ref[...] = -jnp.cos(jnp.pi * codes / 4.0)


def column(s, padded):
    return pl.ds(pl.multiple_of((lax.axis_index("walk") ^ s) * padded, padded), padded)


def place_theta(thetas, theta_s, nocc, width, padded):
    theta_s[...] = jnp.zeros_like(theta_s)
    for w, (ref, n) in enumerate(thetas):
        theta = ref[n] if len(ref.shape) == 3 else ref[...]
        span = theta.shape[1] // 2
        rows = slice(w * LANES, w * LANES + nocc)
        for i in range(2):
            part = theta[i * nocc:(i + 1) * nocc]
            if span == padded:
                theta_s[rows, 2 * i * padded:2 * (i + 1) * padded] = part
            else:
                for k in range(2):
                    lane = (2 * i + k) * padded
                    theta_s[rows, lane:lane + width] = part[:, k * span:k * span + width]


def first_walkers(*refs, first, counts, walkers, half, nocc, width, padded):
    counts = list(counts)
    *thetas, chol_s, weight_ref, same_ref, other_ref, tmat_ref, theta_s, cotan_s = refs
    place_theta([(ref, n) for ref in thetas for n in range(counts.pop(0))], theta_s, nocc, width, padded)
    tmat = lax.dot_general(theta_s[...], chol_s[...], (((1,), (1,)), ((), ())), preferred_element_type=f32)
    tmat_ref[...] = tmat
    n = walkers // 2
    for w in range(walkers):
        row = w // n * (weight_ref.shape[0] // 2) + first + w % n
        weight = weight_ref[row:row + 1, :]
        for g in range(half):
            block = tmat[w * LANES:(w + 1) * LANES, g * LANES:(g + 1) * LANES]
            cotan_s[g * LANES:(g + 1) * LANES, w * LANES:(w + 1) * LANES] = (weight * block).astype(bf16)
    for s, ref in ((2, same_ref), (3, other_ref)):
        ref[...] = jnp.dot(cotan_s[...], theta_s[:, column(s, padded)], preferred_element_type=f32)


def first_energies(tmat_ref, energy_ref, *, half):
    for w in range(energy_ref.shape[0]):
        total = jnp.zeros((LANES, LANES), f32)
        for g in range(half):
            block = tmat_ref[w * LANES:(w + 1) * LANES, g * LANES:(g + 1) * LANES]
            total += block * block.T
        energy_ref[w:w + 1, :] = -0.5 * jnp.sum(total, axis=0, keepdims=True)


def last_walkers(
    mine, theirs, chol_s, weight_ref, same_part, other_part, first_ref, same_ref, other_ref, energy_ref, theta_s, cotan_s,
    *, sources, half, nocc, width, padded
):
    place_theta([(mine, 0), (theirs, 0)], theta_s, nocc, width, padded)
    tmat = lax.dot_general(theta_s[...], chol_s[...], (((1,), (1,)), ((), ())), preferred_element_type=f32)
    for w in range(2):
        row = (w + 1) * (weight_ref.shape[0] // 2) - 1
        weight = weight_ref[row:row + 1, :]
        for g in range(half):
            block = tmat[w * LANES:(w + 1) * LANES, g * LANES:(g + 1) * LANES]
            cotan_s[g * LANES:(g + 1) * LANES, w * LANES:(w + 1) * LANES] = (weight * block).astype(bf16)
    for ref, part, s in ((same_ref, same_part, 2), (other_ref, other_part, 3)):
        grad = part[...] + jnp.dot(cotan_s[...], theta_s[:, column(s, padded)], preferred_element_type=f32)
        store_grad(grad, ref, half, nocc)
    energy_ref[...] = jnp.zeros_like(energy_ref)
    early = first_ref.shape[0] // 2
    me = lax.axis_index("chol")
    rows = [pl.ds(me ^ source_of(me, path), 1) for path in sources]
    for w in range(2):
        total = jnp.zeros((LANES, LANES), f32)
        for g in range(half):
            block = tmat[w * LANES:(w + 1) * LANES, g * LANES:(g + 1) * LANES]
            total += block * block.T
        for n in range(early):
            energy_ref[w, rows[n], :] = first_ref[w * early + n:w * early + n + 1]
        energy_ref[w, rows[early], :] = -0.5 * jnp.sum(total, axis=0, keepdims=True)


def store_grad(grad, ref, half, nocc):
    for g in range(half):
        if len(ref.shape) == 2:
            ref[g * nocc:(g + 1) * nocc] = grad[g * LANES:g * LANES + nocc, :ref.shape[1]].astype(ref.dtype)
        else:
            ref[g] = grad[g * LANES:g * LANES + ref.shape[1]].astype(ref.dtype)


def chip_walkers(*refs, half, nocc, padded):
    *factors, own_ref, low_ref, high_ref = refs
    for s in (1, 0):
        grad = 0.0
        for cotan_s, theta_s in zip(factors[::2], factors[1::2]):
            grad += jnp.dot(cotan_s[...], theta_s[:, column(s, padded)], preferred_element_type=f32)
        if s == 0:
            store_grad(grad, own_ref, half, nocc)
        else:
            store_grad(grad, low_ref, half // 2, nocc)
            store_grad(grad[half // 2 * LANES:], high_ref, half // 2, nocc)


def halve(mine_ref, arrived_ref, keep_ref, send_ref):
    ours, theirs = (ref.at[i] if len(ref.shape) == 3 else ref for i, ref in enumerate((mine_ref, arrived_ref)))
    for n in range(keep_ref.shape[0]):
        for ref, row in ((keep_ref, n), (send_ref, keep_ref.shape[0] + n)):
            ref[n:n + 1, :] = ours[row:row + 1, :] + theirs[row:row + 1, :]


def finish(*refs):
    *refs, out_hbm, energy_hbm, out_ref, energy_ref, sems = refs
    own_ref, same_ref, other_ref, low_ref, high_ref, *energy_refs = refs
    half = own_ref.shape[0]
    nocc, gdev, width = out_ref.shape
    h = lax.rem(lax.axis_index("walk"), 2)
    energy = sum(ref[...] for ref in energy_refs)
    energy_ref[...] = jnp.sum(energy, axis=1, keepdims=True)
    copies = [pltpu.make_async_copy(energy_ref, energy_hbm, sems.at[0])]
    copies[0].start()

    def arrived(*refs):
        n = half // len(refs)
        blocks = [ref[g * nocc + start:g * nocc + stop, :width] for ref in refs for g in range(n)]
        return jnp.stack([block.astype(f32) for block in blocks])

    for n, start in enumerate(range(0, nocc, STEP), start=1):
        stop = min(start + STEP, nocc)
        mine = own_ref[:, start:stop, :width] + arrived(same_ref)
        theirs = arrived(low_ref, high_ref) + arrived(other_ref)

        @pl.when(h == 0)
        def _():
            out_ref[start:stop] = jnp.swapaxes(jnp.concatenate([mine, theirs], axis=0), 0, 1)

        @pl.when(h == 1)
        def _():
            out_ref[start:stop] = jnp.swapaxes(jnp.concatenate([theirs, mine], axis=0), 0, 1)

        copies.append(pltpu.make_async_copy(out_ref.at[start:stop], out_hbm.at[start:stop], sems.at[n]))
        copies[-1].start()
    for copy in copies:
        copy.wait()


def call(kernel, outs, *operands, scratch=(), ins=VMEM, out=VMEM, grant=GRANT):
    return pl.pallas_call(
        kernel,
        out_shape=outs,
        in_specs=[pl.BlockSpec(memory_space=ins)] * len(operands),
        out_specs=jax.tree.map(lambda _: pl.BlockSpec(memory_space=out), outs),
        scratch_shapes=scratch,
        compiler_params=pltpu.CompilerParams(vmem_limit_bytes=grant),
    )(*operands)


def body(chol_vectors, green_blocks, phase_codes, occupations, *, nchol, nwalk):
    gdev, nocc, width = chol_vectors.shape
    norb = green_blocks.shape[3]
    half = gdev // 2
    rows = ceil_to(nocc, 8)
    padded = ceil_to(width, LANES)
    wide = padded * nwalk
    sizes = dict(half=half, padded=padded)

    def swap(x, flip):
        return lax.ppermute(x, "walk", [(i, i ^ flip) for i in range(nwalk)])

    def turn(x, pairs):
        return lax.ppermute(x, "chol", pairs)

    def struct(*shape, dtype=bf16):
        return jax.ShapeDtypeStruct(shape, dtype)

    block = struct(2 * nocc, wide // 2)
    theta, chol_vectors = call(
        functools.partial(prep_theta, width=width, padded=padded),
        (pltpu.VMEM(block.shape, bf16), pltpu.VMEM((nocc, gdev, width), bf16)),
        occupations.reshape(1, nocc),
        green_blocks.reshape(nocc, norb),
        jnp.swapaxes(chol_vectors, 0, 1),
        scratch=[pltpu.VMEM((1, nocc), jnp.int32), pltpu.VMEM((nocc, norb), bf16), pltpu.SemaphoreType.DMA((3,))],
        ins=HBM,
        grant=PREP,
    )
    chol_vectors = jnp.swapaxes(chol_vectors, 0, 1)
    cross = call(prep_chol, struct(2 * nocc + 1, half // 2 * width), chol_vectors, phase_codes)

    if nchol == 4:
        there = [(0, 2), (2, 3), (3, 1), (1, 0)]
        back = [(b, a) for a, b in there]
        paths = [there, back, [(i, 3 - i) for i in range(4)]]
        first = turn(theta, there)
        early = [first, turn(theta, back)]
        last = turn(first, there)
    else:
        paths = [[(i, (i + d) % nchol) for i in range(nchol)] for d in range(1, nchol)]
        *early, last = [turn(theta, path) for path in paths]
    sources = [list(range(nchol))] + [[a for a, _ in sorted(path, key=lambda p: p[1])] for path in paths]

    paired = swap(cross, 1)
    crossed = swap(chol_vectors, 2)
    relayed = swap(call(relay, struct(half, nocc + OPT["rel"], width), crossed), 1)
    chol, weight = call(
        functools.partial(place_chol, sources=sources, nocc=nocc, width=width, **sizes),
        (struct(half * LANES, wide), struct(2 * nchol, LANES, dtype=f32)),
        chol_vectors,
        paired,
        crossed,
        relayed,
        phase_codes,
    )
    term = struct(half * LANES, padded, dtype=f32)
    mine = [theta] + early
    def message(extra, span, *blocks):
        shape = (2 * nocc + extra, 2 * span)
        return call(
            functools.partial(mail, width=width), struct(*shape) if len(blocks) == 1 else struct(2, *shape), *blocks
        )

    a_ops = [swap(message(OPT["ar"], width if OPT["aw"] else padded, theta, early[0]), 1)]
    b_op = message(OPT["br"], width if OPT["bw"] else padded, early[1])
    theirs = a_ops + [swap(b_op, 1)] + [swap(t, 1) for t in early[2:]]
    grads, energies, factors = None, [], []
    for start in range(0, nchol - 1, 3):
        if start == 0 and len(a_ops) == 1:
            group, counts = mine[:3] + theirs[:2], (1, 1, 1, 2, 1)
        else:
            shift = len(a_ops) - 2
            group = mine[start:start + 3] + theirs[start + shift:start + 3 + shift]
            counts = (1,) * len(group)
        walkers = sum(counts)
        *terms, tmat, theta_s, cotan_s = call(
            functools.partial(
                first_walkers, first=start, counts=counts, walkers=walkers, nocc=nocc, width=width, **sizes
            ),
            (
                term,
                term,
                struct(walkers * LANES, half * LANES, dtype=f32),
                struct(walkers * LANES, wide),
                struct(half * LANES, walkers * LANES),
            ),
            *group,
            chol,
            weight,
        )
        energy = call(functools.partial(first_energies, half=half), struct(walkers, LANES, dtype=f32), tmat)
        grads = terms if grads is None else [a + b for a, b in zip(grads, terms)]
        energies += [(energy[:walkers // 2], energy[walkers // 2:])]
        factors += [cotan_s, theta_s]
    if len(energies) > 1:
        energy = jnp.concatenate([e[i] for i in (0, 1) for e in energies])
    theirs_last = swap(lax.optimization_barrier((last, grads[0]))[0], 1)

    walkers = 2
    same, other, energy, theta_s, cotan_s = call(
        functools.partial(last_walkers, sources=sources, nocc=nocc, width=width, **sizes),
        (
            struct(half * nocc, padded),
            struct(half * nocc, width),
            struct(2, nchol + SPARE, LANES, dtype=f32),
            struct(walkers * LANES, wide),
            struct(half * LANES, walkers * LANES),
        ),
        last,
        theirs_last,
        chol,
        weight,
        grads[0],
        grads[1],
        energy,
    )
    same, other = swap(same, 2), swap(other, 3)
    arrived, n = swap(energy, 1), nchol // 2
    while n:
        energy, send = call(halve, (struct(n, LANES, dtype=f32),) * 2, energy, arrived)
        arrived = turn(send, [(i, i ^ n) for i in range(nchol)])
        if n == nchol // 2:
            first_in = arrived
        n //= 2
    own, *core = call(
        functools.partial(chip_walkers, nocc=nocc, **sizes),
        (struct(half, rows, padded, dtype=f32),) + (struct(half // 2 * nocc, width),) * 2,
        *factors,
        cotan_s,
        theta_s,
    )
    core = [swap(c, 1) for c in lax.optimization_barrier((*core, first_in))[:-1]]
    chol_grad, energies = call(
        finish,
        (struct(nocc, gdev, width, dtype=f32), struct(1, 1, dtype=f32)),
        own,
        same,
        other,
        *core,
        energy,
        arrived,
        out=HBM,
        scratch=[
            pltpu.VMEM((nocc, gdev, width), f32),
            pltpu.VMEM((1, 1), f32),
            pltpu.SemaphoreType.DMA((1 - (-nocc // STEP),)),
        ],
    )
    return jnp.swapaxes(chol_grad, 0, 1), energies


def solution(mesh):
    placed = (
        P("chol", None, "walk"),
        P(("dom", "walk"), "chol", None, None),
        P(("dom", "walk"), None),
        P(("dom", "walk"), "chol", None),
    )
    return jax.shard_map(
        functools.partial(body, nchol=mesh.shape["chol"], nwalk=mesh.shape["walk"]),
        mesh=mesh,
        in_specs=placed,
        out_specs=(P(("dom", "chol"), None, "walk"), P(("dom", "walk"), "chol")),
        check_vma=False,
    )
```
